256 devices in a mesh: lat: 16 (over x_hi, y, core), lon: 8 (over z), section: 2 (over x_lo).
Axes of the slice: x: 4 (x_hi: 2, x_lo: 2; x = x_hi * 2 + x_lo), y: 4, z: 8, core: 2. Of those that a mesh axis runs over, the one named last changes fastest.
Arguments:
- fields: bfloat16 [2, 384, 128, 1536], P('section', 'lat', 'lon'), may hold values from -6 to 6, as said below
- land_sea: int32 [384, 128], P('lat', 'lon'), may hold values 0 or 1
- pole_valid: int32 [384, 128], P('lat', 'lon'), may hold values from 0 to 1, as said below
- lead_steps: int32 [2, 2], P('section'), may hold values from 0 to 39
- lead_table: float32 [40, 1536], replicated, may hold values from -3 to 3
- land_vector: float32 [1536], replicated, may hold values from -3 to 3
- norm_gain: float32 [2, 1536], P('section'), may hold values from 0.1 to 1.9
- w_query: bfloat16 [2, 1536, 768], P('section'), may hold values from -0.15309311 to 0.15309311
- w_key: bfloat16 [2, 1536, 768], P('section'), may hold values from -0.20412415 to 0.20412415
- w_value: bfloat16 [2, 1536, 768], P('section'), may hold values from -0.15625 to 0.15625
- w_out: bfloat16 [2, 768, 1536], P('section'), may hold values from -0.21875 to 0.21875
- logit_scale: float32 [2, 12], P('section'), may hold values from 2 to 400
Outputs:
- rollout: bfloat16 [2, 384, 128, 1536], P('section', 'lat', 'lon')
The draws below stay inside these ranges and needn't reach their ends.
Inputs may be any that keep to these rules, and one draw needn't show every extreme that they name: `fields`: each initial time's state; entries of order one. `pole_valid`: in each longitude column, 0 on its own number of first latitude rows and its own number of last latitude rows, each number 1 to 6, and 1 elsewhere; some column has 6 on both sides.
All inputs are finite; a program needn't handle non-finite values. No bound on the sum of `land_sea` on one device may be relied on, other than what follows from the above.
Results may differ from the reference program's by a relative error of at most 0.007.
Values may be sent and summed in bfloat16 or wider, within the bound.
A program may use at most 128 MiB of HBM per device.

```python
import math
import jax
import jax.numpy as jnp
from jax import lax

D = 1536
HEADS = 12
HEAD_DIM = 64
RADIUS = 6
LEADS = 40
CLAT = 24
CLON = 16
NLAT = 384
NLON = 128


def shared_projection(key):
    return jnp.clip(jax.random.normal(key, (2, D, HEADS * HEAD_DIM), jnp.float32), -6.0, 6.0)


def draw_w_query(key, part):
    shared = shared_projection(key)
    return (shared * D ** (-0.5)).astype(jnp.bfloat16)


def draw_w_key(key, part):
    shared = shared_projection(key)
    key = jax.random.fold_in(key, 5)
    private = jnp.clip(jax.random.normal(key, shared.shape, jnp.float32), -6.0, 6.0)
    mixed = 0.6 * shared + 0.8 * private
    return (mixed * D ** (-0.5)).astype(jnp.bfloat16)


def draw_logit_scale(key, part):
    key = jax.random.fold_in(key, 7)
    fraction = jax.random.uniform(key, (2, HEADS), jnp.float32)
    lower, upper = (2.0, 12.0)
    return jnp.exp(math.log(lower) + fraction * (math.log(upper) - math.log(lower)))


def draw_fields(key, part):
    key = jax.random.fold_in(key, 11)
    first_key = jax.random.fold_in(key, 0)
    rough = jnp.clip(jax.random.normal(first_key, (2, NLAT, NLON, D), jnp.float32), -6.0, 6.0)
    values = rough
    return values.astype(jnp.bfloat16)


def draw_pole_valid(key, part):
    key = jax.random.fold_in(key, 13)
    first_key, second_key, third_key = jax.random.split(key, 3)
    north = jax.random.randint(first_key, (NLON,), 1, RADIUS + 1, jnp.int32)
    south = jax.random.randint(second_key, (NLON,), 1, RADIUS + 1, jnp.int32)
    deepest = jax.random.randint(third_key, (), 0, NLON, jnp.int32)
    column_index = jnp.arange(NLON, dtype=jnp.int32)
    north = jnp.where(column_index == deepest, RADIUS, north)
    south = jnp.where(column_index == deepest, RADIUS, south)
    row_index = jnp.broadcast_to(jnp.arange(NLAT, dtype=jnp.int32)[:, None], (NLAT, NLON))
    inside = (row_index >= north[None, :]) & (row_index < NLAT - south[None, :])
    return jnp.where(inside, 1, 0).astype(jnp.int32)


def set_ends(values, own_key, smallest, largest):
    longest = values.shape.index(max(values.shape))
    spots = []
    for shift in (0, 1):
        where = [jax.random.randint(jax.random.fold_in(own_key, axis), (), 0, length) for axis, length in enumerate(values.shape)]
        where[longest] = (where[longest] + shift) % values.shape[longest]
        spots.append(tuple(where))
    return values.at[spots[0]].set(smallest).at[spots[1]].set(largest)


def levels(own_key, dims, shards, smallest, largest):
    level, own = 1.0, jax.random.fold_in(own_key, 6)
    for position, blocks in shards:
        draws = jnp.exp(jax.random.uniform(jax.random.fold_in(own, position), (blocks,), jnp.float32, smallest / len(shards), largest / len(shards)))
        level = level * jnp.repeat(draws, dims[position] // blocks).reshape([-1 if axis == position else 1 for axis in range(len(dims))])
    return level


def bell_draw(key, dims, deviation, most, shards=(), kind=jnp.bfloat16):
    loudness = levels(key, dims, shards, -0.22, 0.18) if shards else 1.0
    result = jax.random.normal(key, dims, jnp.float32) * deviation * loudness
    return jnp.minimum(jnp.maximum(result, -most), most).astype(kind)


def setup_inputs(seed: int = 0) -> dict:
    arg_keys = jax.random.split(jax.random.key(seed), 13)
    fields = draw_fields(jax.random.fold_in(arg_keys[12], 71), 0)
    land_sea = set_ends((jax.random.randint(arg_keys[1], (NLAT, NLON), 0, 10) < 3).astype(jnp.int32), jax.random.fold_in(arg_keys[1], 1), 0, 1)
    pole_valid = draw_pole_valid(jax.random.fold_in(arg_keys[12], 71), 0)
    lead_steps = set_ends(jax.random.randint(arg_keys[3], (2, 2), 0, LEADS), jax.random.fold_in(arg_keys[3], 1), 0, LEADS - 1).astype(jnp.int32)
    lead_table = bell_draw(arg_keys[4], (LEADS, D), 0.5, 3.0, (), jnp.float32)
    land_vector = bell_draw(arg_keys[5], (D,), 0.5, 3.0, (), jnp.float32)
    norm_gain = jnp.clip(1.0 + 0.18 * jax.random.normal(arg_keys[6], (2, D), jnp.float32), 0.1, 1.9)
    w_query = draw_w_query(jax.random.fold_in(arg_keys[12], 71), 0)
    w_key = draw_w_key(jax.random.fold_in(arg_keys[12], 71), 0)
    w_value = bell_draw(arg_keys[9], (2, D, HEADS * HEAD_DIM), D ** -0.5, 0.15625, ((0, 2),))
    w_out = bell_draw(arg_keys[10], (2, HEADS * HEAD_DIM, D), (HEADS * HEAD_DIM) ** -0.5, 0.21875, ((0, 2),))
    logit_scale = draw_logit_scale(jax.random.fold_in(arg_keys[12], 71), 0)
    return dict(fields=fields, land_sea=land_sea, pole_valid=pole_valid, lead_steps=lead_steps, lead_table=lead_table, land_vector=land_vector, norm_gain=norm_gain, w_query=w_query, w_key=w_key, w_value=w_value, w_out=w_out, logit_scale=logit_scale)


def lead_row(table, index):
    hits = jnp.arange(table.shape[0], dtype=jnp.int32) == index
    return lax.optimization_barrier(jnp.sum(jnp.where(hits[:, None], table, 0.0), axis=0))

def admitted(cell_rows, cell_cols, reach, valid_pad):
    query_rows = jnp.repeat(jnp.arange(cell_rows, dtype=jnp.int32), cell_cols)
    query_cols = jnp.tile(jnp.arange(cell_cols, dtype=jnp.int32), cell_rows)
    wide_rows = cell_rows + 2 * reach
    wide_cols = cell_cols + 2 * reach
    key_rows = jnp.repeat(jnp.arange(wide_rows, dtype=jnp.int32), wide_cols)
    key_cols = jnp.tile(jnp.arange(wide_cols, dtype=jnp.int32), wide_rows)
    near_rows = jnp.abs(key_rows[None, :] - query_rows[:, None] - reach) <= reach
    near_cols = jnp.abs(key_cols[None, :] - query_cols[:, None] - reach) <= reach
    usable = valid_pad.reshape(-1)[None, :] == 1
    return near_rows & near_cols & usable

def attend_tile(query_unit, padded, valid_pad, tau):
    cell_rows, cell_cols, head_count, head_size = query_unit.shape
    inner = head_count * head_size
    mask = admitted(cell_rows, cell_cols, RADIUS, valid_pad)
    keys = padded.reshape(-1, 2 * inner)
    key_part = keys[:, :inner].reshape(-1, head_count, head_size).astype(jnp.float32)
    value_part = keys[:, inner:].reshape(-1, head_count, head_size).astype(jnp.float32)
    query_flat = query_unit.reshape(-1, head_count, head_size).astype(jnp.float32)
    scores = jnp.einsum('qhd,khd->hqk', query_flat, key_part) * (tau / head_size)[:, None, None]
    highest = lax.optimization_barrier(jnp.max(jnp.where(mask[None], scores, -jnp.inf), axis=-1, keepdims=True))
    prob = jnp.where(mask[None], jnp.exp(scores - highest), 0.0)
    denom = lax.optimization_barrier(jnp.sum(prob, axis=-1))
    weights = prob.astype(jnp.bfloat16).astype(jnp.float32)
    numer = jnp.einsum('hqk,khd->qhd', weights, value_part)
    attended = numer / jnp.transpose(denom)[:, :, None]
    return attended.reshape(cell_rows, cell_cols, inner).astype(jnp.bfloat16)

def layer(grid, land_sea, valid_pad, land_vector, lead_vec, gain, tau, wq, wk, wv, wo):
    grid_rows, grid_cols, width = grid.shape
    head_count = tau.shape[0]
    inner = wq.shape[1]
    head_size = inner // head_count
    cond = grid.astype(jnp.float32) + lead_vec + land_sea[:, :, None].astype(jnp.float32) * land_vector
    mean_square = lax.optimization_barrier(jnp.mean(cond * cond, axis=-1, keepdims=True))
    normed = (cond * lax.rsqrt(mean_square + 1e-05) * gain).astype(jnp.bfloat16)
    flat = normed.reshape(-1, width)
    query = jnp.dot(flat, wq, preferred_element_type=jnp.float32).reshape(-1, head_count, head_size)
    keyproj = jnp.dot(flat, wk, preferred_element_type=jnp.float32).reshape(-1, head_count, head_size)
    query_unit = (query * lax.rsqrt(lax.optimization_barrier(jnp.mean(query * query, axis=-1, keepdims=True)) + 1e-06)).astype(jnp.bfloat16)
    key_unit = (keyproj * lax.rsqrt(lax.optimization_barrier(jnp.mean(keyproj * keyproj, axis=-1, keepdims=True)) + 1e-06)).astype(jnp.bfloat16)
    value = jnp.dot(flat, wv, preferred_element_type=jnp.float32).astype(jnp.bfloat16)
    packed = jnp.concatenate([key_unit.reshape(-1, inner), value], axis=-1).reshape(grid_rows, grid_cols, 2 * inner)
    packed = jnp.concatenate([packed[:, grid_cols - RADIUS:], packed, packed[:, :RADIUS]], axis=1)
    packed = jnp.pad(packed, ((RADIUS, RADIUS), (0, 0), (0, 0)))
    query_grid = query_unit.reshape(grid_rows, grid_cols, head_count, head_size)
    tile_rows = grid_rows // CLAT
    tile_cols = grid_cols // CLON
    zero_index = jnp.zeros((), jnp.int32)

    def one_tile(index):
        row_start = (index // tile_cols * CLAT).astype(jnp.int32)
        col_start = (index % tile_cols * CLON).astype(jnp.int32)
        query_tile = lax.dynamic_slice(query_grid, (row_start, col_start, zero_index, zero_index), (CLAT, CLON, head_count, head_size))
        key_tile = lax.dynamic_slice(packed, (row_start, col_start, zero_index), (CLAT + 2 * RADIUS, CLON + 2 * RADIUS, 2 * inner))
        valid_tile = lax.dynamic_slice(valid_pad, (row_start, col_start), (CLAT + 2 * RADIUS, CLON + 2 * RADIUS))
        return attend_tile(query_tile, key_tile, valid_tile, tau)
    tiles = lax.map(one_tile, jnp.arange(tile_rows * tile_cols, dtype=jnp.int32))
    attended = tiles.reshape(tile_rows, tile_cols, CLAT, CLON, inner).transpose(0, 2, 1, 3, 4).reshape(-1, inner)
    projected = jnp.dot(attended, wo, preferred_element_type=jnp.float32).reshape(grid_rows, grid_cols, width)
    return (grid.astype(jnp.float32) + projected).astype(jnp.bfloat16)

def reference(fields, land_sea, pole_valid, lead_steps, lead_table, land_vector, norm_gain, w_query, w_key, w_value, w_out, logit_scale):
    grid_cols = pole_valid.shape[1]
    valid_pad = jnp.concatenate([pole_valid[:, grid_cols - RADIUS:], pole_valid, pole_valid[:, :RADIUS]], axis=1)
    valid_pad = jnp.pad(valid_pad, ((RADIUS, RADIUS), (0, 0)))

    def apply_section(section_index, grid, lead_index):
        return layer(grid, land_sea, valid_pad, land_vector, lead_row(lead_table, lead_index), norm_gain[section_index], logit_scale[section_index], w_query[section_index], w_key[section_index], w_value[section_index], w_out[section_index])
    first_zero = apply_section(0, fields[0], lead_steps[0, 0])
    first_one = apply_section(1, fields[1], lead_steps[1, 0])
    final_zero = apply_section(0, first_one, lead_steps[0, 1])
    final_one = apply_section(1, first_zero, lead_steps[1, 1])
    return jnp.stack([final_zero, final_one], axis=0)
```

```python
import functools

import jax
import jax.numpy as jnp
from jax import lax
from jax.experimental import pallas as pl
from jax.experimental.pallas import tpu as pltpu
from jax.sharding import PartitionSpec as P

R = 6
ROWS = 24
COLS = 16
CELLS = ROWS * COLS
D = 1536
INNER = 768
HEADS = 12
HEAD = 64
LANES = 256
GROUPS = INNER // LANES
PER_GROUP = LANES // HEAD
PROWS = 8
PCELLS = PROWS * COLS
PIECES = ROWS // PROWS
BROWS = 4
BCELLS = BROWS * COLS
BLOCKS = ROWS // BROWS
STRIP = PROWS * R
OWN = (ROWS + 2 * R) * COLS
SIDE = (ROWS + 2 * PROWS) * R
REACH = 112
SPARE = 32
WIDE = 128
LOG2E = 1.4426950408889634
LOW = -1e30
F32 = jnp.float32
BF16 = jnp.bfloat16

Z_LEFT = 0
Z_RIGHT = PIECES
EDGE = 2 * PIECES
SLOTS = EDGE + 6


def dot_t(a, b):
    return lax.dot_general(a, b, (((1,), (1,)), ((), ())), preferred_element_type=F32)


def dot(a, b):
    return jnp.dot(a, b, preferred_element_type=F32)


def iota(shape, dim):
    return lax.broadcasted_iota(jnp.int32, shape, dim)


def cell_column(grid, row, col, cells):
    picks = (iota((cells, grid.shape[0]), 1) == row).astype(F32).astype(BF16)
    rows = dot(picks, grid.astype(BF16))
    hit = iota(rows.shape, 1) == col
    return jnp.sum(jnp.where(hit, rows, 0.0), axis=1, keepdims=True)


def key_flags(row, col, valid, cells):
    lane = iota((cells, WIDE), 1)
    hit = (lane == row) | (lane == col + 48)
    flags = jnp.where(lane == 100, valid, jnp.where(hit, 1.0, 0.0))
    return flags.astype(BF16)


def kernel(
    lat_count,
    lon_count,
    lead_steps,
    logit_scale,
    fields,
    land_sea,
    pole_valid,
    lead_table,
    land_vector,
    norm_gain,
    w_query,
    w_key,
    w_value,
    w_out,
    out,
    x_buf,
    state,
    wq,
    wk,
    wv,
    wo,
    query,
    own,
    left,
    right,
    strips,
    flag_own,
    flag_left,
    flag_right,
    land,
    attended,
    ones_block,
    pole_mine,
    pole_side,
    load_sem,
    out_sem,
    send_sem,
    recv_sem,
    sec_send,
    sec_recv,
    pole_send,
    pole_recv,
):
    lat = lax.axis_index("lat")
    lon = lax.axis_index("lon")
    sec = lax.axis_index("section")
    west = lax.rem(lon + lon_count - 1, lon_count)
    east = lax.rem(lon + 1, lon_count)
    other = 1 - sec
    flip = lax.rem(lat, 2)
    has_up = lat > 0
    has_down = lat < lat_count - 1
    early = lat - 1 + 2 * flip
    late = lat + 1 - 2 * flip
    has_early = jnp.where(flip == 0, has_up, has_down)
    has_late = jnp.where(flip == 0, has_down, has_up)

    loads = [
        pltpu.make_async_copy(src, dst, load_sem.at[i])
        for i, (src, dst) in enumerate(
            (
                (fields, x_buf.at[0]),
                (w_query, wq),
                (w_key, wk),
                (w_value, wv),
                (w_out, wo),
            )
        )
    ]
    for load in loads:
        load.start()

    for buf in (left, right):
        for l in (0, 1):
            buf[l, pl.ds(0, STRIP), :] = jnp.zeros((STRIP, D), BF16)
            buf[l, pl.ds(192, SIDE - 192), :] = jnp.zeros((SIDE - 192, D), BF16)
    for l in (0, 1):
        own[l, pl.ds(0, R * COLS), :] = jnp.zeros((R * COLS, D), BF16)
        own[l, pl.ds(OWN - R * COLS, R * COLS), :] = jnp.zeros((R * COLS, D), BF16)
    pole_mine[...] = jnp.zeros((ROWS, 128), F32)
    pole_mine[:, pl.ds(0, COLS)] = pole_valid[...].astype(F32)

    barrier = pltpu.get_barrier_semaphore()
    pl.semaphore_signal(barrier, inc=1, device_id={"lon": west})
    pl.semaphore_signal(barrier, inc=1, device_id={"lon": east})
    pl.semaphore_signal(barrier, inc=1, device_id={"section": other})

    @pl.when(has_early)
    def _():
        pl.semaphore_signal(barrier, inc=1, device_id={"lat": early})

    @pl.when(has_late)
    def _():
        pl.semaphore_signal(barrier, inc=1, device_id={"lat": late})

    pl.semaphore_wait(barrier, 3 + has_early.astype(jnp.int32) + has_late.astype(jnp.int32))

    def remote(src, dst, send, recv, device):
        return pltpu.make_async_remote_copy(
            src_ref=src, dst_ref=dst, send_sem=send, recv_sem=recv, device_id=device
        )

    def piece_at(p):
        return p + flip * (PIECES - 1 - 2 * p)

    def block_at(i):
        return i + flip * (BLOCKS - 1 - 2 * i)

    pole_copies = (
        remote(pole_mine, pole_side.at[1], pole_send.at[0], pole_recv.at[0], {"lon": west}),
        remote(pole_mine, pole_side.at[0], pole_send.at[1], pole_recv.at[1], {"lon": east}),
    )
    for copy in pole_copies:
        copy.start()

    def z_copies(l, p):
        c = piece_at(p)
        src = pl.ds(pl.multiple_of(c * STRIP, 16), STRIP)
        dst = pl.ds(pl.multiple_of((c + 1) * STRIP, 16), STRIP)
        return (
            remote(
                strips.at[l, 0, src],
                right.at[l, dst],
                send_sem.at[l, Z_LEFT + p],
                recv_sem.at[l, Z_LEFT + p],
                {"lon": west},
            ),
            remote(
                strips.at[l, 1, src],
                left.at[l, dst],
                send_sem.at[l, Z_RIGHT + p],
                recv_sem.at[l, Z_RIGHT + p],
                {"lon": east},
            ),
        )

    def edge_copies(l, which, parts):
        upper = flip if which else 1 - flip
        device = {"lat": late if which else early}
        base = EDGE + 3 * which
        o_src = pl.multiple_of((1 - upper) * (CELLS - R * COLS) + R * COLS, 16)
        o_dst = pl.multiple_of(upper * (OWN - R * COLS), 16)
        s_src = pl.multiple_of(STRIP + (1 - upper) * (PIECES - 1) * STRIP, 16)
        s_dst = pl.multiple_of(upper * (PIECES + 1) * STRIP, 16)
        copies = []
        for j in parts:
            buf = (own, left, right)[j]
            src, dst, size = (o_src, o_dst, R * COLS) if j == 0 else (s_src, s_dst, STRIP)
            copies.append(
                remote(
                    buf.at[l, pl.ds(src, size)],
                    buf.at[l, pl.ds(dst, size)],
                    send_sem.at[l, base + j],
                    recv_sem.at[l, base + j],
                    device,
                )
            )
        return copies

    def edge_when(which, act):
        pl.when(has_late if which else has_early)(act)

    def start_edge_own(l, which):
        def act():
            edge_copies(l, which, (0,))[0].start()

        edge_when(which, act)

    def start_edge_sides(l, which):
        def act():
            for copy in edge_copies(l, which, (1, 2)):
                copy.start()

        edge_when(which, act)

    def wait_edges(l, which):
        upper = flip if which else 1 - flip
        base = EDGE + 3 * which
        o_dst = pl.multiple_of((1 - upper) * (OWN - R * COLS), 16)
        s_dst = pl.multiple_of((1 - upper) * (PIECES + 1) * STRIP, 16)

        def act():
            device = {"lat": late if which else early}
            for j, (buf, start, size) in enumerate(
                ((own, o_dst, R * COLS), (left, s_dst, STRIP), (right, s_dst, STRIP))
            ):
                ref = buf.at[l, pl.ds(start, size)]
                remote(
                    ref, ref, send_sem.at[l, base + j], recv_sem.at[l, base + j], device
                ).wait_recv()

        edge_when(which, act)

    def wait_z(l, p):
        for copy in z_copies(l, p):
            copy.wait_recv()

    def section_copy(i):
        rows = pl.ds(pl.multiple_of(block_at(i) * BCELLS, BCELLS), BCELLS)
        return remote(
            state.at[rows], x_buf.at[1, rows], sec_send.at[i], sec_recv.at[i], {"section": other}
        )

    def out_copy(i):
        rows = pl.ds(pl.multiple_of(block_at(i) * BCELLS, BCELLS), BCELLS)
        return pltpu.make_async_copy(state.at[rows], out.at[rows], out_sem.at[i])

    cell = iota((CELLS, 1), 0)
    land[...] = cell_column(
        land_sea[...].astype(F32), lax.shift_right_logical(cell, 4), cell & 15, CELLS
    )
    same = lax.shift_right_logical(iota((LANES, LANES), 0), 6) == lax.shift_right_logical(
        iota((LANES, LANES), 1), 6
    )
    ones_block[...] = jnp.where(same, 1.0, 0.0).astype(BF16)

    up_flag = has_up.astype(F32)
    down_flag = has_down.astype(F32)

    def build_flags():
        cell = iota((OWN, 1), 0)
        row = lax.shift_right_logical(cell, 4)
        col = cell & 15
        inside = cell_column(pole_mine[...], row - R, col, OWN)
        valid = jnp.where(row < R, up_flag, jnp.where(row >= R + ROWS, down_flag, inside))
        flag_own[...] = key_flags(row, col + R, valid, OWN)
        cell = iota((SIDE, 1), 0)
        row = jnp.floor((cell.astype(F32) + 0.5) * (1.0 / R)).astype(jnp.int32)
        col = cell - R * row
        row = row - (PROWS - R)
        for s, ref in ((0, flag_left), (1, flag_right)):
            picked = col + (COLS - R if s == 0 else 0)
            inside = cell_column(pole_side[s], row - R, picked, SIDE)
            valid = jnp.where(row < R, up_flag, jnp.where(row >= R + ROWS, down_flag, inside))
            ref[...] = key_flags(row, col + (0 if s == 0 else R + COLS), valid, SIDE)

    def unit(x):
        parts = []
        for t in range(GROUPS):
            part = x[:, t * LANES : (t + 1) * LANES]
            square = part * part
            high = square.astype(BF16)
            low = (square - high.astype(F32)).astype(BF16)
            total = dot(high, ones_block[...]) + dot(low, ones_block[...])
            parts.append((part * lax.rsqrt(total * (1.0 / HEAD) + 1e-06)).astype(BF16))
        return jnp.concatenate(parts, axis=1)

    pick_row = iota((2 * STRIP, PCELLS), 0)
    pick_cell = iota((2 * STRIP, PCELLS), 1)
    pick_side = (pick_row >= STRIP).astype(jnp.int32)
    pick_row = pick_row - STRIP * pick_side
    pick_line = jnp.floor((pick_row.astype(F32) + 0.5) * (1.0 / R)).astype(jnp.int32)
    target = pick_line * COLS + (pick_row - R * pick_line) + (COLS - R) * pick_side
    pick = jnp.where(pick_cell == target, 1.0, 0.0).astype(BF16)

    lead_index = iota((lead_table.shape[0], 1), 0)
    lead_rows = [
        jnp.sum(
            jnp.where(lead_index == lead_steps[0, l], lead_table[...], 0.0), axis=0, keepdims=True
        )
        for l in (0, 1)
    ]

    def project(l, p):
        c = piece_at(p)
        rows = pl.ds(pl.multiple_of(c * PCELLS, PCELLS), PCELLS)
        cond = (
            x_buf[l, rows, :].astype(F32) + lead_rows[l] + land[rows, :] * land_vector[...]
        )
        mean_square = jnp.mean(cond * cond, axis=1, keepdims=True)
        normed = (cond * lax.rsqrt(mean_square + 1e-05) * norm_gain[...]).astype(BF16)
        inner_rows = pl.ds(pl.multiple_of(c * PCELLS + R * COLS, 16), PCELLS)
        strip_rows = pl.ds(pl.multiple_of(c * STRIP, 16), STRIP)

        def finish(part, lanes):
            own[l, inner_rows, lanes] = part
            sent = dot(pick, part).astype(BF16)
            strips[l, 0, strip_rows, lanes] = sent[:STRIP]
            strips[l, 1, strip_rows, lanes] = sent[STRIP:]

        finish(unit(dot(normed, wk[...])), pl.ds(0, INNER))
        finish(dot(normed, wv[...]).astype(BF16), pl.ds(INNER, INNER))
        for copy in z_copies(l, p):
            copy.start()
        query[rows, :] = unit(dot(normed, wq[...]))

    def attend(l, i):
        b = block_at(i)
        rows = pl.ds(pl.multiple_of(b * BCELLS, BCELLS), BCELLS)
        own_rows = pl.ds(pl.multiple_of(b * BCELLS, BCELLS), 16 * COLS)
        side_rows = pl.ds(
            pl.multiple_of(16 * lax.shift_right_logical(6 * b + 3, 2), 16), REACH
        )
        spare = jnp.zeros((SPARE, LANES), BF16)
        q_cell = iota((BCELLS, WIDE), 0)
        lane = iota((BCELLS, WIDE), 1)
        q_row = lax.shift_right_logical(q_cell, 4) + b * BROWS
        q_col = q_cell & 15
        near_row = (lane >= q_row) & (lane <= q_row + 2 * R)
        near_col = (lane - 48 >= q_col) & (lane - 48 <= q_col + 2 * R)
        wanted = jnp.where(near_row | near_col | (lane == 100), 1.0, 0.0).astype(BF16)
        flags = jnp.concatenate(
            [flag_own[own_rows, :], flag_left[side_rows, :], flag_right[side_rows, :], spare[:, :WIDE]], axis=0
        )
        bias = jnp.where(dot_t(wanted, flags) > 2.5, 0.0, LOW)
        lane_head = lax.shift_right_logical(iota((1, LANES), 1), 6)
        for g in range(GROUPS):
            k_lanes = pl.ds(g * LANES, LANES)
            v_lanes = pl.ds(INNER + g * LANES, LANES)
            q = query[rows, k_lanes]
            q_all = jnp.concatenate(
                [
                    jnp.where(lane_head == h, q, jnp.zeros_like(q))
                    for h in range(PER_GROUP)
                ],
                axis=0,
            )
            keys = jnp.concatenate(
                [
                    own[l, own_rows, k_lanes],
                    left[l, side_rows, k_lanes],
                    right[l, side_rows, k_lanes],
                    spare,
                ],
                axis=0,
            )
            values = jnp.concatenate(
                [
                    own[l, own_rows, v_lanes],
                    left[l, side_rows, v_lanes],
                    right[l, side_rows, v_lanes],
                    spare,
                ],
                axis=0,
            )
            scores = dot_t(q_all, keys)
            probs = []
            inverses = []
            for h in range(PER_GROUP):
                factor = logit_scale[0, g * PER_GROUP + h] * (LOG2E / HEAD)
                part = scores[h * BCELLS : (h + 1) * BCELLS] * factor + bias
                prob = jnp.exp2(part - jnp.max(part, axis=1, keepdims=True))
                inverses.append(1.0 / jnp.sum(prob, axis=1, keepdims=True))
                probs.append(prob.astype(BF16))
            mixed = dot(jnp.concatenate(probs, axis=0), values)
            total = jnp.zeros((BCELLS, LANES), F32)
            for h in range(PER_GROUP):
                part = mixed[h * BCELLS : (h + 1) * BCELLS] * inverses[h]
                total = jnp.where(lane_head == h, part, total)
            attended[:, k_lanes] = total.astype(BF16)
        moved = x_buf[l, rows, :].astype(F32) + dot(attended[...], wo[...])
        state[rows, :] = moved.astype(BF16)

    def project_loop(l, low, high):
        def body(p, carry):
            project(l, p)
            return carry

        lax.fori_loop(low, high, body, 0)

    for load in loads[:4]:
        load.wait()
    project_loop(0, 0, 1)
    start_edge_own(0, 0)
    project_loop(0, 1, PIECES)
    start_edge_own(0, 1)
    loads[4].wait()
    for copy in pole_copies:
        copy.wait_recv()
    build_flags()
    wait_z(0, 0)
    start_edge_sides(0, 0)
    wait_z(0, 1)
    wait_edges(0, 0)

    def first_body(i, carry):
        @pl.when(i == 2)
        def _():
            wait_z(0, 2)
            start_edge_sides(0, 1)

        @pl.when(i == 4)
        def _():
            wait_edges(0, 1)

        attend(0, i)
        section_copy(i).start()
        return carry

    lax.fori_loop(0, BLOCKS, first_body, 0)

    for i in (0, 1):
        section_copy(i).wait_recv()
    project_loop(1, 0, 1)
    start_edge_own(1, 0)
    for i in (2, 3):
        section_copy(i).wait_recv()
    project_loop(1, 1, 2)
    for i in range(BLOCKS):
        section_copy(i).wait_send()
    wait_z(1, 0)
    start_edge_sides(1, 0)
    wait_z(1, 1)
    wait_edges(1, 0)

    def second_body(i, carry):
        @pl.when(i == 2)
        def _():
            for j in (4, 5):
                section_copy(j).wait_recv()
            project(1, 2)
            start_edge_own(1, 1)
            wait_z(1, 2)
            start_edge_sides(1, 1)

        @pl.when(i == 4)
        def _():
            wait_edges(1, 1)

        attend(1, i)
        out_copy(i).start()
        return carry

    lax.fori_loop(0, BLOCKS, second_body, 0)

    for i in range(BLOCKS):
        out_copy(i).wait()
    for copy in pole_copies:
        copy.wait_send()
    for l in (0, 1):
        for p in range(PIECES):
            for copy in z_copies(l, p):
                copy.wait_send()
        for which in (0, 1):

            def act(l=l, which=which):
                for copy in edge_copies(l, which, (0, 1, 2)):
                    copy.wait_send()

            edge_when(which, act)


def per_device(
    lat_count,
    lon_count,
    fields,
    land_sea,
    pole_valid,
    lead_steps,
    lead_table,
    land_vector,
    norm_gain,
    w_query,
    w_key,
    w_value,
    w_out,
    logit_scale,
):
    vmem = pl.BlockSpec(memory_space=pltpu.VMEM)
    smem = pl.BlockSpec(memory_space=pltpu.SMEM)
    hbm = pl.BlockSpec(memory_space=pl.ANY)
    result = pl.pallas_call(
        functools.partial(kernel, lat_count, lon_count),
        out_shape=jax.ShapeDtypeStruct((CELLS, D), BF16),
        in_specs=[smem, smem, hbm, vmem, vmem, vmem, vmem, vmem, hbm, hbm, hbm, hbm],
        out_specs=hbm,
        scratch_shapes=[
            pltpu.VMEM((2, CELLS, D), BF16),
            pltpu.VMEM((CELLS, D), BF16),
            pltpu.VMEM((D, INNER), BF16),
            pltpu.VMEM((D, INNER), BF16),
            pltpu.VMEM((D, INNER), BF16),
            pltpu.VMEM((INNER, D), BF16),
            pltpu.VMEM((CELLS, INNER), BF16),
            pltpu.VMEM((2, OWN, D), BF16),
            pltpu.VMEM((2, SIDE, D), BF16),
            pltpu.VMEM((2, SIDE, D), BF16),
            pltpu.VMEM((2, 2, PIECES * STRIP, D), BF16),
            pltpu.VMEM((OWN, WIDE), BF16),
            pltpu.VMEM((SIDE, WIDE), BF16),
            pltpu.VMEM((SIDE, WIDE), BF16),
            pltpu.VMEM((CELLS, 1), F32),
            pltpu.VMEM((BCELLS, INNER), BF16),
            pltpu.VMEM((LANES, LANES), BF16),
            pltpu.VMEM((ROWS, 128), F32),
            pltpu.VMEM((2, ROWS, 128), F32),
            pltpu.SemaphoreType.DMA((5,)),
            pltpu.SemaphoreType.DMA((BLOCKS,)),
            pltpu.SemaphoreType.DMA((2, SLOTS)),
            pltpu.SemaphoreType.DMA((2, SLOTS)),
            pltpu.SemaphoreType.DMA((BLOCKS,)),
            pltpu.SemaphoreType.DMA((BLOCKS,)),
            pltpu.SemaphoreType.DMA((2,)),
            pltpu.SemaphoreType.DMA((2,)),
        ],
        compiler_params=pltpu.CompilerParams(
            collective_id=0, has_side_effects=True, vmem_limit_bytes=56 * 1024 * 1024
        ),
    )(
        lead_steps,
        logit_scale,
        fields.reshape(CELLS, D),
        land_sea,
        pole_valid,
        lead_table,
        land_vector.reshape(1, D),
        norm_gain,
        w_query[0],
        w_key[0],
        w_value[0],
        w_out[0],
    )
    return result.reshape(1, ROWS, COLS, D)


def solution(mesh):
    return jax.shard_map(
        functools.partial(per_device, mesh.shape["lat"], mesh.shape["lon"]),
        mesh=mesh,
        in_specs=(
            P("section", "lat", "lon", None),
            P("lat", "lon"),
            P("lat", "lon"),
            P("section", None),
            P(),
            P(),
            P("section", None),
            P("section", None, None),
            P("section", None, None),
            P("section", None, None),
            P("section", None, None),
            P("section", None),
        ),
        out_specs=P("section", "lat", "lon", None),
        check_vma=False,
    )
```

```python
import functools

import jax
import jax.numpy as jnp
from jax import lax
from jax.experimental import pallas as pl
from jax.experimental.pallas import tpu as pltpu
from jax.sharding import PartitionSpec as P

R = 6
ROWS = 24
COLS = 16
CELLS = ROWS * COLS
D = 1536
INNER = 768
HEADS = 12
HEAD = 64
LANES = 256
GROUPS = INNER // LANES
PER_GROUP = LANES // HEAD
PROWS = 8
PCELLS = PROWS * COLS
PIECES = ROWS // PROWS
BROWS = 4
BCELLS = BROWS * COLS
BLOCKS = ROWS // BROWS
STRIP = PROWS * R
OWN = (ROWS + 2 * R) * COLS
SIDE = (ROWS + 2 * PROWS) * R
REACH = 112
SPARE = 32
WIDE = 128
LOG2E = 1.4426950408889634
LOW = -1e30
F32 = jnp.float32
BF16 = jnp.bfloat16

PARTS = PIECES + 2
EDGE = 2 * PARTS
SLOTS = EDGE + 6


def dot_t(a, b):
    return lax.dot_general(a, b, (((1,), (1,)), ((), ())), preferred_element_type=F32)


def dot(a, b):
    return jnp.dot(a, b, preferred_element_type=F32)


def iota(shape, dim):
    return lax.broadcasted_iota(jnp.int32, shape, dim)


def cell_column(grid, row, col, cells):
    picks = (iota((cells, grid.shape[0]), 1) == col).astype(F32).astype(BF16)
    found = dot(picks, grid.astype(BF16))
    hit = iota(found.shape, 1) == row
    return jnp.sum(jnp.where(hit, found, 0.0), axis=1, keepdims=True)


def key_flags(row, col, valid, cells):
    lane = iota((cells, WIDE), 1)
    hit = (lane == row) | (lane == col + 48)
    flags = jnp.where(lane == 100, valid, jnp.where(hit, 1.0, 0.0))
    return flags.astype(BF16)


def kernel(
    lat_count,
    lon_count,
    lead_steps,
    logit_scale,
    fields,
    land_sea_in,
    pole_valid_in,
    lead_table_in,
    land_vector_in,
    norm_gain_in,
    w_query,
    w_key,
    w_value,
    w_out,
    out,
    land_sea,
    pole_valid,
    lead_table,
    land_vector,
    norm_gain,
    x_buf,
    state,
    final,
    normed,
    wq,
    wk,
    wv,
    wo,
    query,
    own,
    left,
    right,
    strips,
    flag_own,
    flag_left,
    flag_right,
    land,
    attended,
    ones_block,
    pole_mine,
    pole_side,
    corners,
    small_sem,
    load_sem,
    out_sem,
    send_sem,
    recv_sem,
    sec_send,
    sec_recv,
    pole_send,
    pole_recv,
):
    lat = lax.axis_index("lat")
    lon = lax.axis_index("lon")
    sec = lax.axis_index("section")
    west = lax.rem(lon + lon_count - 1, lon_count)
    east = lax.rem(lon + 1, lon_count)
    other = 1 - sec
    flip = lax.rem(lat, 2)
    has_up = lat > 0
    has_down = lat < lat_count - 1
    early = lat - 1 + 2 * flip
    late = lat + 1 - 2 * flip
    has_early = jnp.where(flip == 0, has_up, has_down)
    has_late = jnp.where(flip == 0, has_down, has_up)

    barrier = pltpu.get_barrier_semaphore()
    pl.semaphore_signal(barrier, inc=1, device_id={"lon": west})
    pl.semaphore_signal(barrier, inc=1, device_id={"lon": east})
    pl.semaphore_signal(barrier, inc=1, device_id={"section": other})

    @pl.when(has_early)
    def _():
        pl.semaphore_signal(barrier, inc=1, device_id={"lat": early})

    @pl.when(has_late)
    def _():
        pl.semaphore_signal(barrier, inc=1, device_id={"lat": late})

    def piece_at(p):
        return p + flip * (PIECES - 1 - 2 * p)

    def block_at(i):
        return i + flip * (BLOCKS - 1 - 2 * i)

    def load_piece(p):
        rows = pl.ds(pl.multiple_of(piece_at(p) * PCELLS, PCELLS), PCELLS)
        return pltpu.make_async_copy(fields.at[rows], x_buf.at[0, rows], load_sem.at[p])

    load_key = pltpu.make_async_copy(w_key, wk, load_sem.at[PIECES])
    load_value = pltpu.make_async_copy(w_value, wv, load_sem.at[PIECES + 1])
    load_query = pltpu.make_async_copy(w_query, wq, load_sem.at[PIECES + 2])
    load_out = pltpu.make_async_copy(w_out, wo, load_sem.at[PIECES + 3])
    load_piece(0).start()
    smalls = [
        pltpu.make_async_copy(src, dst, small_sem.at[i])
        for i, (src, dst) in enumerate(
            (
                (lead_table_in, lead_table),
                (land_vector_in, land_vector),
                (norm_gain_in, norm_gain),
                (land_sea_in, land_sea),
                (pole_valid_in, pole_valid),
            )
        )
    ]
    for small in smalls:
        small.start()
    load_key.start()
    load_value.start()
    for p in range(1, PIECES):
        load_piece(p).start()

    def clear_rows(missing, own_start, side_start):
        @pl.when(missing)
        def _():
            for l in (0, 1):
                own[l, pl.ds(own_start, R * COLS), :] = jnp.zeros((R * COLS, D), BF16)
                for buf in (left, right):
                    buf[l, pl.ds(side_start, STRIP), :] = jnp.zeros((STRIP, D), BF16)

    clear_rows(jnp.logical_not(has_up), 0, 0)
    clear_rows(jnp.logical_not(has_down), OWN - R * COLS, SIDE - STRIP)
    for small in smalls:
        small.wait()
    pole_mine[...] = jnp.zeros((COLS, 128), F32)
    pole_mine[:, pl.ds(0, ROWS)] = pole_valid[...].astype(F32)

    def remote(src, dst, send, recv, device):
        return pltpu.make_async_remote_copy(
            src_ref=src, dst_ref=dst, send_sem=send, recv_sem=recv, device_id=device
        )

    pole_copies = (
        remote(pole_mine, pole_side.at[1], pole_send.at[0], pole_recv.at[0], {"lon": west}),
        remote(pole_mine, pole_side.at[0], pole_send.at[1], pole_recv.at[1], {"lon": east}),
    )
    def part_at(p):
        if isinstance(p, int) and p >= PIECES:
            base = piece_at(PIECES - 1) * STRIP
            if p == PIECES:
                return base + flip * 32, 16
            return base + (1 - flip) * 16, 32
        return piece_at(p) * STRIP, STRIP

    def z_copies(l, p):
        start, size = part_at(p)
        src = pl.ds(pl.multiple_of(start, 16), size)
        dst = pl.ds(pl.multiple_of(start + STRIP, 16), size)
        return (
            remote(
                strips.at[l, 0, src],
                right.at[l, dst],
                send_sem.at[l, p],
                recv_sem.at[l, p],
                {"lon": west},
            ),
            remote(
                strips.at[l, 1, src],
                left.at[l, dst],
                send_sem.at[l, PARTS + p],
                recv_sem.at[l, PARTS + p],
                {"lon": east},
            ),
        )

    def start_z(l, p):
        for copy in z_copies(l, p):
            copy.start()

    def edge_copies(l, which, parts):
        upper = flip if which else 1 - flip
        device = {"lat": late if which else early}
        base = EDGE + 3 * which
        o_src = pl.multiple_of((1 - upper) * (CELLS - R * COLS) + R * COLS, 16)
        o_dst = pl.multiple_of(upper * (OWN - R * COLS), 16)
        s_src = pl.multiple_of(STRIP + (1 - upper) * (PIECES - 1) * STRIP, 16)
        s_dst = pl.multiple_of(upper * (PIECES + 1) * STRIP, 16)
        copies = []
        for j in parts:
            buf = (own, left, right)[j]
            src, dst, size = (o_src, o_dst, R * COLS) if j == 0 else (s_src, s_dst, STRIP)
            copies.append(
                remote(
                    buf.at[l, pl.ds(src, size)],
                    buf.at[l, pl.ds(dst, size)],
                    send_sem.at[l, base + j],
                    recv_sem.at[l, base + j],
                    device,
                )
            )
        return copies

    def edge_when(which, act):
        pl.when(has_late if which else has_early)(act)

    def start_edge_own(l, which):
        def act():
            edge_copies(l, which, (0,))[0].start()

        edge_when(which, act)

    def start_late_sides(l):
        def act():
            for copy in edge_copies(l, 1, (1, 2)):
                copy.start()

        edge_when(1, act)

    def corner_copies(l):
        rows = pl.ds(pl.multiple_of(flip * (SIDE - STRIP), 16), STRIP)
        return (
            remote(
                corners.at[l, 0],
                right.at[l, rows],
                send_sem.at[l, EDGE + 1],
                recv_sem.at[l, EDGE + 1],
                {"lon": west},
            ),
            remote(
                corners.at[l, 1],
                left.at[l, rows],
                send_sem.at[l, EDGE + 2],
                recv_sem.at[l, EDGE + 2],
                {"lon": east},
            ),
        )

    def start_corners(l):
        def act():
            start = flip * (OWN - R * COLS)
            rows = pl.ds(pl.multiple_of(start, 16), R * COLS)
            ref = own.at[l, rows]
            remote(
                ref, ref, send_sem.at[l, EDGE], recv_sem.at[l, EDGE], {"lat": early}
            ).wait_recv()
            picked = picker(0, STRIP, R * COLS, (1 - flip) * (PROWS - R) * COLS)
            for lanes in (pl.ds(0, INNER), pl.ds(INNER, INNER)):
                sent = dot(picked, own[l, rows, lanes]).astype(BF16)
                corners[l, 0, :, lanes] = sent[:STRIP]
                corners[l, 1, :, lanes] = sent[STRIP:]
            for copy in corner_copies(l):
                copy.start()

        edge_when(0, act)

    def wait_corners(l):
        def act():
            for copy in corner_copies(l):
                copy.wait_recv()

        edge_when(0, act)

    def wait_late(l):
        o_dst = pl.multiple_of((1 - flip) * (OWN - R * COLS), 16)
        s_dst = pl.multiple_of((1 - flip) * (SIDE - STRIP), 16)

        def act():
            for j, (buf, start, size) in enumerate(
                ((own, o_dst, R * COLS), (left, s_dst, STRIP), (right, s_dst, STRIP))
            ):
                ref = buf.at[l, pl.ds(start, size)]
                remote(
                    ref,
                    ref,
                    send_sem.at[l, EDGE + 3 + j],
                    recv_sem.at[l, EDGE + 3 + j],
                    {"lat": late},
                ).wait_recv()

        edge_when(1, act)

    def wait_z(l, p):
        for copy in z_copies(l, p):
            copy.wait_recv()

    def section_copy(i):
        rows = pl.ds(pl.multiple_of(block_at(i) * BCELLS, BCELLS), BCELLS)
        return remote(
            state.at[rows], x_buf.at[1, rows], sec_send.at[i], sec_recv.at[i], {"section": other}
        )

    def out_copy(i):
        rows = pl.ds(pl.multiple_of(block_at(i) * BCELLS, BCELLS), BCELLS)
        return pltpu.make_async_copy(final.at[rows], out.at[rows], out_sem.at[i])

    cell = iota((CELLS, 1), 0)
    land[...] = cell_column(
        land_sea[...].astype(F32), lax.shift_right_logical(cell, 4), cell & 15, CELLS
    )
    same = lax.shift_right_logical(iota((LANES, LANES), 0), 6) == lax.shift_right_logical(
        iota((LANES, LANES), 1), 6
    )
    ones_block[...] = jnp.where(same, 1.0, 0.0).astype(BF16)

    up_flag = has_up.astype(F32)
    down_flag = has_down.astype(F32)

    def build_flags():
        cell = iota((OWN, 1), 0)
        row = lax.shift_right_logical(cell, 4)
        col = cell & 15
        inside = cell_column(pole_mine[...], row - R, col, OWN)
        valid = jnp.where(row < R, up_flag, jnp.where(row >= R + ROWS, down_flag, inside))
        flag_own[...] = key_flags(row, col + R, valid, OWN)
        cell = iota((SIDE, 1), 0)
        row = jnp.floor((cell.astype(F32) + 0.5) * (1.0 / R)).astype(jnp.int32)
        col = cell - R * row
        row = row - (PROWS - R)
        for s, ref in ((0, flag_left), (1, flag_right)):
            picked = col + (COLS - R if s == 0 else 0)
            inside = cell_column(pole_side[s], row - R, picked, SIDE)
            valid = jnp.where(row < R, up_flag, jnp.where(row >= R + ROWS, down_flag, inside))
            ref[...] = key_flags(row, col + (0 if s == 0 else R + COLS), valid, SIDE)

    def unit(x):
        parts = []
        for t in range(GROUPS):
            part = x[:, t * LANES : (t + 1) * LANES]
            square = part * part
            high = square.astype(BF16)
            low = (square - high.astype(F32)).astype(BF16)
            total = dot(high, ones_block[...]) + dot(low, ones_block[...])
            parts.append((part * lax.rsqrt(total * (1.0 / HEAD) + 1e-06)).astype(BF16))
        return jnp.concatenate(parts, axis=1)

    def picker(first, count, cells, first_cell):
        line = iota((2 * count, cells), 0)
        side = (line >= count).astype(jnp.int32)
        strip_cell = line - count * side + first
        row = jnp.floor((strip_cell.astype(F32) + 0.5) * (1.0 / R)).astype(jnp.int32)
        wanted = row * COLS + (strip_cell - R * row) + (COLS - R) * side - first_cell
        return jnp.where(iota((2 * count, cells), 1) == wanted, 1.0, 0.0).astype(BF16)

    pick = picker(0, STRIP, PCELLS, 0)

    land_row = land_vector[...].reshape(1, D)
    lead_index = iota((lead_table.shape[0], 1), 0)
    lead_rows = [
        jnp.sum(
            jnp.where(lead_index == lead_steps[0, l], lead_table[...], 0.0), axis=0, keepdims=True
        )
        for l in (0, 1)
    ]

    def store_strips(l, picked, start, count, part, lanes):
        sent = dot(picked, part).astype(BF16)
        rows = pl.ds(pl.multiple_of(start, 16), count)
        strips[l, 0, rows, lanes] = sent[:count]
        strips[l, 1, rows, lanes] = sent[count:]

    def keys_values(l, start, size, done, before_value=lambda: None):
        rows = pl.ds(pl.multiple_of(start, BCELLS), size)
        cond = x_buf[l, rows, :].astype(F32) + lead_rows[l] + land[rows, :] * land_row
        mean_square = jnp.mean(cond * cond, axis=1, keepdims=True)
        flat = (cond * lax.rsqrt(mean_square + 1e-05) * norm_gain[...]).astype(BF16)
        normed[rows, :] = flat
        inner_rows = pl.ds(pl.multiple_of(start + R * COLS, 16), size)
        for weight, lanes in ((wk, pl.ds(0, INNER)), (wv, pl.ds(INNER, INNER))):
            if weight is wv:
                before_value()
            part = dot(flat, weight[...])
            part = unit(part) if weight is wk else part.astype(BF16)
            own[l, inner_rows, lanes] = part
            done(part, lanes)

    def piece_keys_values(l, p):
        c = piece_at(p)

        def done(part, lanes):
            store_strips(l, pick, c * STRIP, STRIP, part, lanes)

        def before_value():
            if l == 0:
                pl.when(p == 0)(load_value.wait)

        keys_values(l, c * PCELLS, PCELLS, done, before_value)
        if l == 0:
            pl.when(p < PIECES - 1)(lambda: start_z(l, p))
        else:
            start_z(l, p)

    def queries(start, size):
        rows = pl.ds(pl.multiple_of(start, BCELLS), size)
        query[rows, :] = unit(dot(normed[rows, :], wq[...]))

    def attend(l, i):
        b = block_at(i)
        rows = pl.ds(pl.multiple_of(b * BCELLS, BCELLS), BCELLS)
        own_rows = pl.ds(pl.multiple_of(b * BCELLS, BCELLS), 16 * COLS)
        side_rows = pl.ds(
            pl.multiple_of(16 * lax.shift_right_logical(6 * b + 3, 2), 16), REACH
        )
        spare = jnp.zeros((SPARE, LANES), BF16)
        q_cell = iota((BCELLS, WIDE), 0)
        lane = iota((BCELLS, WIDE), 1)
        q_row = lax.shift_right_logical(q_cell, 4) + b * BROWS
        q_col = q_cell & 15
        near_row = (lane >= q_row) & (lane <= q_row + 2 * R)
        near_col = (lane - 48 >= q_col) & (lane - 48 <= q_col + 2 * R)
        wanted = jnp.where(near_row | near_col | (lane == 100), 1.0, 0.0).astype(BF16)
        flags = jnp.concatenate(
            [flag_own[own_rows, :], flag_left[side_rows, :], flag_right[side_rows, :], spare[:, :WIDE]], axis=0
        )
        bias = jnp.where(dot_t(wanted, flags) > 2.5, 0.0, LOW)
        lane_head = lax.shift_right_logical(iota((1, LANES), 1), 6)
        for g in range(GROUPS):
            k_lanes = pl.ds(g * LANES, LANES)
            v_lanes = pl.ds(INNER + g * LANES, LANES)
            q = query[rows, k_lanes]
            q_all = jnp.concatenate(
                [
                    jnp.where(lane_head == h, q, jnp.zeros_like(q))
                    for h in range(PER_GROUP)
                ],
                axis=0,
            )
            keys = jnp.concatenate(
                [
                    own[l, own_rows, k_lanes],
                    left[l, side_rows, k_lanes],
                    right[l, side_rows, k_lanes],
                    spare,
                ],
                axis=0,
            )
            values = jnp.concatenate(
                [
                    own[l, own_rows, v_lanes],
                    left[l, side_rows, v_lanes],
                    right[l, side_rows, v_lanes],
                    spare,
                ],
                axis=0,
            )
            scores = dot_t(q_all, keys)
            probs = []
            inverses = []
            for h in range(PER_GROUP):
                factor = logit_scale[0, g * PER_GROUP + h] * (LOG2E / HEAD)
                part = scores[h * BCELLS : (h + 1) * BCELLS] * factor + bias
                prob = jnp.exp2(part - jnp.max(part, axis=1, keepdims=True))
                inverses.append(1.0 / jnp.sum(prob, axis=1, keepdims=True))
                probs.append(prob.astype(BF16))
            mixed = dot(jnp.concatenate(probs, axis=0), values)
            total = jnp.zeros((BCELLS, LANES), F32)
            for h in range(PER_GROUP):
                part = mixed[h * BCELLS : (h + 1) * BCELLS] * inverses[h]
                total = jnp.where(lane_head == h, part, total)
            attended[rows, k_lanes] = total.astype(BF16)

    def project_out(l, start, size):
        rows = pl.ds(pl.multiple_of(start, BCELLS), size)
        moved = x_buf[l, rows, :].astype(F32) + dot(attended[rows, :], wo[...])
        (state if l == 0 else final)[rows, :] = moved.astype(BF16)

    def order(i):
        return lax.rem(i + 2, 4) + 2 * lax.shift_right_logical(i, 2)

    load_key.wait()

    def first_project(p, carry):
        load_piece(p).wait()

        @pl.when(p == 1)
        def _():
            start_edge_own(0, 0)
            load_query.start()
            load_out.start()

        piece_keys_values(0, p)
        return carry

    pl.semaphore_wait(barrier, 3 + has_early.astype(jnp.int32) + has_late.astype(jnp.int32))
    lax.fori_loop(0, PIECES, first_project, 0)
    start_z(0, PIECES)
    start_z(0, PIECES + 1)
    start_edge_own(0, 1)
    for copy in pole_copies:
        copy.start()
    load_query.wait()

    def first_query(p, carry):
        queries(piece_at(p) * PCELLS, PCELLS)
        return carry

    lax.fori_loop(0, PIECES, first_query, 0)
    start_corners(0)
    load_out.wait()
    for copy in pole_copies:
        copy.wait_recv()
    build_flags()
    wait_z(0, 0)
    wait_z(0, 1)
    wait_z(0, PIECES)

    def first_body(i, carry):
        block = order(i)

        @pl.when(i == 1)
        def _():
            wait_z(0, PIECES + 1)
            start_late_sides(0)

        @pl.when(i == 2)
        def _():
            wait_corners(0)

        @pl.when(i == 4)
        def _():
            wait_late(0)

        attend(0, block)

        @pl.when(i < 2)
        def _():
            project_out(0, block_at(block) * BCELLS, BCELLS)
            section_copy(block).start()

        @pl.when((i == 3) | (i == 5))
        def _():
            project_out(0, piece_at(lax.shift_right_logical(block, 1)) * PCELLS, PCELLS)
            section_copy(block - 1).start()
            section_copy(block).start()

        return carry

    lax.fori_loop(0, BLOCKS, first_body, 0)

    def second_project(step, carry):
        p = 1 - step
        section_copy(2 * p).wait_recv()
        section_copy(2 * p + 1).wait_recv()
        piece_keys_values(1, p)

        @pl.when(step == 1)
        def _():
            start_edge_own(1, 0)

        queries(piece_at(p) * PCELLS, PCELLS)
        return carry

    lax.fori_loop(0, PIECES - 1, second_project, 0)

    def last_piece():
        c = piece_at(PIECES - 1)
        section_copy(4).wait_recv()
        block = block_at(4)
        start, count = part_at(PIECES)
        half = (block - 2 * c) * BCELLS
        picked = picker(start - c * STRIP, count, BCELLS, half)

        def done(part, lanes):
            store_strips(1, picked, start, count, part, lanes)

        keys_values(1, block * BCELLS, BCELLS, done)
        start_z(1, PIECES)
        queries(block * BCELLS, BCELLS)
        start_corners(1)

        section_copy(5).wait_recv()
        block = block_at(5)
        start, count = part_at(PIECES + 1)
        picked = picker(start - c * STRIP, count, PCELLS, 0)
        keys_values(1, block * BCELLS, BCELLS, lambda part, lanes: None)
        rows = pl.ds(pl.multiple_of(c * PCELLS + R * COLS, 16), PCELLS)
        for lanes in (pl.ds(0, INNER), pl.ds(INNER, INNER)):
            store_strips(1, picked, start, count, own[1, rows, lanes], lanes)
        start_z(1, PIECES + 1)
        start_edge_own(1, 1)
        queries(block * BCELLS, BCELLS)

    half_cells = CELLS // 2

    def second_body(i, carry):
        block = lax.rem(i + 2, 3) + 3 * lax.div(i, 3)
        block = jnp.where(i < 3, block, i)

        @pl.when(i == 1)
        def _():
            wait_corners(1)

        @pl.when(i == 3)
        def _():
            project_out(1, flip * half_cells, half_cells)
            for j in range(3):
                out_copy(j).start()
            wait_z(1, PIECES + 1)
            start_late_sides(1)

        @pl.when(i == 4)
        def _():
            wait_late(1)

        attend(1, block)
        return carry

    last_piece()
    wait_z(1, 1)
    wait_z(1, 0)
    wait_z(1, PIECES)
    lax.fori_loop(0, BLOCKS, second_body, 0)
    project_out(1, (1 - flip) * half_cells, half_cells)
    for j in range(3, BLOCKS):
        out_copy(j).start()

    for copy in pole_copies:
        copy.wait_send()
    for i in range(BLOCKS):
        section_copy(i).wait_send()
    for l in (0, 1):
        for p in (0, 1, PIECES, PIECES + 1):
            for copy in z_copies(l, p):
                copy.wait_send()

        def early_sent(l=l):
            edge_copies(l, 0, (0,))[0].wait_send()
            for copy in corner_copies(l):
                copy.wait_send()

        def late_sent(l=l):
            for copy in edge_copies(l, 1, (0, 1, 2)):
                copy.wait_send()

        edge_when(0, early_sent)
        edge_when(1, late_sent)
    for i in range(BLOCKS):
        out_copy(i).wait()


def per_device(
    lat_count,
    lon_count,
    fields,
    land_sea,
    pole_valid,
    lead_steps,
    lead_table,
    land_vector,
    norm_gain,
    w_query,
    w_key,
    w_value,
    w_out,
    logit_scale,
):
    smem = pl.BlockSpec(memory_space=pltpu.SMEM)
    hbm = pl.BlockSpec(memory_space=pl.ANY)
    result = pl.pallas_call(
        functools.partial(kernel, lat_count, lon_count),
        out_shape=jax.ShapeDtypeStruct((CELLS, D), BF16),
        in_specs=[smem, smem] + [hbm] * 10,
        out_specs=hbm,
        scratch_shapes=[
            pltpu.VMEM((COLS, ROWS), jnp.int32),
            pltpu.VMEM((COLS, ROWS), jnp.int32),
            pltpu.VMEM(lead_table.shape, F32),
            pltpu.VMEM(land_vector.shape, F32),
            pltpu.VMEM(norm_gain.shape, F32),
            pltpu.VMEM((2, CELLS, D), BF16),
            pltpu.VMEM((CELLS, D), BF16),
            pltpu.VMEM((CELLS, D), BF16),
            pltpu.VMEM((CELLS, D), BF16),
            pltpu.VMEM((D, INNER), BF16),
            pltpu.VMEM((D, INNER), BF16),
            pltpu.VMEM((D, INNER), BF16),
            pltpu.VMEM((INNER, D), BF16),
            pltpu.VMEM((CELLS, INNER), BF16),
            pltpu.VMEM((2, OWN, D), BF16),
            pltpu.VMEM((2, SIDE, D), BF16),
            pltpu.VMEM((2, SIDE, D), BF16),
            pltpu.VMEM((2, 2, PIECES * STRIP, D), BF16),
            pltpu.VMEM((OWN, WIDE), BF16),
            pltpu.VMEM((SIDE, WIDE), BF16),
            pltpu.VMEM((SIDE, WIDE), BF16),
            pltpu.VMEM((CELLS, 1), F32),
            pltpu.VMEM((CELLS, INNER), BF16),
            pltpu.VMEM((LANES, LANES), BF16),
            pltpu.VMEM((COLS, 128), F32),
            pltpu.VMEM((2, COLS, 128), F32),
            pltpu.VMEM((2, 2, STRIP, D), BF16),
            pltpu.SemaphoreType.DMA((5,)),
            pltpu.SemaphoreType.DMA((PIECES + 4,)),
            pltpu.SemaphoreType.DMA((BLOCKS,)),
            pltpu.SemaphoreType.DMA((2, SLOTS)),
            pltpu.SemaphoreType.DMA((2, SLOTS)),
            pltpu.SemaphoreType.DMA((BLOCKS,)),
            pltpu.SemaphoreType.DMA((BLOCKS,)),
            pltpu.SemaphoreType.DMA((2,)),
            pltpu.SemaphoreType.DMA((2,)),
        ],
        compiler_params=pltpu.CompilerParams(
            collective_id=0, has_side_effects=True, vmem_limit_bytes=56 * 1024 * 1024
        ),
    )(
        lead_steps,
        logit_scale,
        fields.reshape(CELLS, D),
        land_sea.T,
        pole_valid.T,
        lead_table,
        land_vector,
        norm_gain,
        w_query[0],
        w_key[0],
        w_value[0],
        w_out[0],
    )
    return result.reshape(1, ROWS, COLS, D)


def solution(mesh):
    return jax.shard_map(
        functools.partial(per_device, mesh.shape["lat"], mesh.shape["lon"]),
        mesh=mesh,
        in_specs=(
            P("section", "lat", "lon", None),
            P("lat", "lon"),
            P("lat", "lon"),
            P("section", None),
            P(),
            P(),
            P("section", None),
            P("section", None, None),
            P("section", None, None),
            P("section", None, None),
            P("section", None, None),
            P("section", None),
        ),
        out_specs=P("section", "lat", "lon", None),
        check_vma=False,
    )
```

```python
import functools

import jax
import jax.numpy as jnp
from jax import lax
from jax.experimental import pallas as pl
from jax.experimental.pallas import tpu as pltpu
from jax.sharding import PartitionSpec as P

R = 6
ROWS = 24
COLS = 16
CELLS = ROWS * COLS
D = 1536
INNER = 768
HEADS = 12
HEAD = 64
LANES = 256
GROUPS = INNER // LANES
PER_GROUP = LANES // HEAD
PROWS = 8
PCELLS = PROWS * COLS
PIECES = ROWS // PROWS
BROWS = 4
BCELLS = BROWS * COLS
BLOCKS = ROWS // BROWS
STRIP = PROWS * R
OWN = (ROWS + 2 * R) * COLS
SIDE = (ROWS + 2 * PROWS) * R
REACH = 112
SPARE = 32
WIDE = 128
LOG2E = 1.4426950408889634
LOW = -1e30
F32 = jnp.float32
BF16 = jnp.bfloat16

PARTS = PIECES + 2
EDGE = 2 * PARTS
SLOTS = EDGE + 6


def dot_t(a, b):
    return lax.dot_general(a, b, (((1,), (1,)), ((), ())), preferred_element_type=F32)


def dot(a, b):
    return jnp.dot(a, b, preferred_element_type=F32)


def iota(shape, dim):
    return lax.broadcasted_iota(jnp.int32, shape, dim)


def cell_column(grid, row, col, cells):
    picks = (iota((cells, grid.shape[0]), 1) == col).astype(F32).astype(BF16)
    found = dot(picks, grid.astype(BF16))
    hit = iota(found.shape, 1) == row
    return jnp.sum(jnp.where(hit, found, 0.0), axis=1, keepdims=True)


def key_flags(row, col, valid, cells):
    lane = iota((cells, WIDE), 1)
    hit = (lane == row) | (lane == col + 48)
    flags = jnp.where(lane == 100, valid, jnp.where(hit, 1.0, 0.0))
    return flags.astype(BF16)


def kernel(
    lat_count,
    lon_count,
    lead_steps,
    logit_scale,
    fields,
    land_sea_in,
    pole_valid_in,
    lead_table_in,
    land_vector_in,
    norm_gain_in,
    w_query,
    w_key,
    w_value,
    w_out,
    out,
    land_sea,
    pole_valid,
    lead_table,
    land_vector,
    norm_gain,
    x_buf,
    state,
    final,
    normed,
    wq,
    wk,
    wv,
    wo,
    query,
    own,
    left,
    right,
    strips,
    flag_own,
    flag_left,
    flag_right,
    land,
    attended,
    ones_block,
    pole_mine,
    pole_side,
    corners,
    small_sem,
    load_sem,
    out_sem,
    send_sem,
    recv_sem,
    sec_send,
    sec_recv,
    pole_send,
    pole_recv,
):
    lat = lax.axis_index("lat")
    lon = lax.axis_index("lon")
    sec = lax.axis_index("section")
    west = lax.rem(lon + lon_count - 1, lon_count)
    east = lax.rem(lon + 1, lon_count)
    other = 1 - sec
    flip = lax.rem(lat, 2)
    has_up = lat > 0
    has_down = lat < lat_count - 1
    early = lat - 1 + 2 * flip
    late = lat + 1 - 2 * flip
    has_early = jnp.where(flip == 0, has_up, has_down)
    has_late = jnp.where(flip == 0, has_down, has_up)

    barrier = pltpu.get_barrier_semaphore()
    pl.semaphore_signal(barrier, inc=1, device_id={"lon": west})
    pl.semaphore_signal(barrier, inc=1, device_id={"lon": east})
    pl.semaphore_signal(barrier, inc=1, device_id={"section": other})

    @pl.when(has_early)
    def _():
        pl.semaphore_signal(barrier, inc=1, device_id={"lat": early})

    @pl.when(has_late)
    def _():
        pl.semaphore_signal(barrier, inc=1, device_id={"lat": late})

    def piece_at(p):
        return p + flip * (PIECES - 1 - 2 * p)

    def block_at(i):
        return i + flip * (BLOCKS - 1 - 2 * i)

    def load_piece(p):
        rows = pl.ds(pl.multiple_of(piece_at(p) * PCELLS, PCELLS), PCELLS)
        return pltpu.make_async_copy(fields.at[rows], x_buf.at[0, rows], load_sem.at[p])

    load_key = pltpu.make_async_copy(w_key, wk, load_sem.at[PIECES])
    load_value = pltpu.make_async_copy(w_value, wv, load_sem.at[PIECES + 1])
    load_query = pltpu.make_async_copy(w_query, wq, load_sem.at[PIECES + 2])
    load_out = pltpu.make_async_copy(w_out, wo, load_sem.at[PIECES + 3])
    load_piece(0).start()
    smalls = [
        pltpu.make_async_copy(src, dst, small_sem.at[i])
        for i, (src, dst) in enumerate(
            (
                (lead_table_in, lead_table),
                (land_vector_in, land_vector),
                (norm_gain_in, norm_gain),
                (land_sea_in, land_sea),
                (pole_valid_in, pole_valid),
            )
        )
    ]
    for small in smalls:
        small.start()
    load_key.start()
    load_value.start()
    for p in range(1, PIECES):
        load_piece(p).start()

    def clear_rows(missing, own_start, side_start):
        @pl.when(missing)
        def _():
            for l in (0, 1):
                own[l, pl.ds(own_start, R * COLS), :] = jnp.zeros((R * COLS, D), BF16)
                for buf in (left, right):
                    buf[l, pl.ds(side_start, STRIP), :] = jnp.zeros((STRIP, D), BF16)

    clear_rows(jnp.logical_not(has_up), 0, 0)
    clear_rows(jnp.logical_not(has_down), OWN - R * COLS, SIDE - STRIP)
    for small in smalls:
        small.wait()
    pole_mine[...] = jnp.zeros((COLS, 128), F32)
    pole_mine[:, pl.ds(0, ROWS)] = pole_valid[...].astype(F32)

    def remote(src, dst, send, recv, device):
        return pltpu.make_async_remote_copy(
            src_ref=src, dst_ref=dst, send_sem=send, recv_sem=recv, device_id=device
        )

    pole_copies = (
        remote(pole_mine, pole_side.at[1], pole_send.at[0], pole_recv.at[0], {"lon": west}),
        remote(pole_mine, pole_side.at[0], pole_send.at[1], pole_recv.at[1], {"lon": east}),
    )
    def part_at(p):
        if isinstance(p, int) and p >= PIECES:
            base = piece_at(PIECES - 1) * STRIP
            if p == PIECES:
                return base + flip * 32, 16
            return base + (1 - flip) * 16, 32
        return piece_at(p) * STRIP, STRIP

    def z_copies(l, p):
        start, size = part_at(p)
        src = pl.ds(pl.multiple_of(start, 16), size)
        dst = pl.ds(pl.multiple_of(start + STRIP, 16), size)
        return (
            remote(
                strips.at[l, 0, src],
                right.at[l, dst],
                send_sem.at[l, p],
                recv_sem.at[l, p],
                {"lon": west},
            ),
            remote(
                strips.at[l, 1, src],
                left.at[l, dst],
                send_sem.at[l, PARTS + p],
                recv_sem.at[l, PARTS + p],
                {"lon": east},
            ),
        )

    def start_z(l, p):
        for copy in z_copies(l, p):
            copy.start()

    def sent_z(l, p):
        for copy in z_copies(l, p):
            copy.wait_send()

    def edge_copies(l, which, parts):
        upper = flip if which else 1 - flip
        device = {"lat": late if which else early}
        base = EDGE + 3 * which
        o_src = pl.multiple_of((1 - upper) * (CELLS - R * COLS) + R * COLS, 16)
        o_dst = pl.multiple_of(upper * (OWN - R * COLS), 16)
        s_src = pl.multiple_of(STRIP + (1 - upper) * (PIECES - 1) * STRIP, 16)
        s_dst = pl.multiple_of(upper * (PIECES + 1) * STRIP, 16)
        copies = []
        for j in parts:
            buf = (own, left, right)[j]
            src, dst, size = (o_src, o_dst, R * COLS) if j == 0 else (s_src, s_dst, STRIP)
            copies.append(
                remote(
                    buf.at[l, pl.ds(src, size)],
                    buf.at[l, pl.ds(dst, size)],
                    send_sem.at[l, base + j],
                    recv_sem.at[l, base + j],
                    device,
                )
            )
        return copies

    def edge_when(which, act):
        pl.when(has_late if which else has_early)(act)

    def start_edge_own(l, which):
        def act():
            edge_copies(l, which, (0,))[0].start()

        edge_when(which, act)

    def start_late_sides(l):
        def act():
            for copy in edge_copies(l, 1, (1, 2)):
                copy.start()

        edge_when(1, act)

    def corner_copies(l):
        rows = pl.ds(pl.multiple_of(flip * (SIDE - STRIP), 16), STRIP)
        return (
            remote(
                corners.at[l, 0],
                right.at[l, rows],
                send_sem.at[l, EDGE + 1],
                recv_sem.at[l, EDGE + 1],
                {"lon": west},
            ),
            remote(
                corners.at[l, 1],
                left.at[l, rows],
                send_sem.at[l, EDGE + 2],
                recv_sem.at[l, EDGE + 2],
                {"lon": east},
            ),
        )

    def start_corners(l):
        def act():
            start = flip * (OWN - R * COLS)
            rows = pl.ds(pl.multiple_of(start, 16), R * COLS)
            ref = own.at[l, rows]
            remote(
                ref, ref, send_sem.at[l, EDGE], recv_sem.at[l, EDGE], {"lat": early}
            ).wait_recv()
            picked = picker(0, STRIP, R * COLS, (1 - flip) * (PROWS - R) * COLS)
            for lanes in (pl.ds(0, INNER), pl.ds(INNER, INNER)):
                sent = dot(picked, own[l, rows, lanes]).astype(BF16)
                corners[l, 0, :, lanes] = sent[:STRIP]
                corners[l, 1, :, lanes] = sent[STRIP:]
            for copy in corner_copies(l):
                copy.start()

        edge_when(0, act)

    def wait_corners(l):
        def act():
            for copy in corner_copies(l):
                copy.wait_recv()

        edge_when(0, act)

    def wait_late(l):
        o_dst = pl.multiple_of((1 - flip) * (OWN - R * COLS), 16)
        s_dst = pl.multiple_of((1 - flip) * (SIDE - STRIP), 16)

        def act():
            for j, (buf, start, size) in enumerate(
                ((own, o_dst, R * COLS), (left, s_dst, STRIP), (right, s_dst, STRIP))
            ):
                ref = buf.at[l, pl.ds(start, size)]
                remote(
                    ref,
                    ref,
                    send_sem.at[l, EDGE + 3 + j],
                    recv_sem.at[l, EDGE + 3 + j],
                    {"lat": late},
                ).wait_recv()

        edge_when(1, act)

    def wait_z(l, p):
        for copy in z_copies(l, p):
            copy.wait_recv()

    def section_copy(i):
        rows = pl.ds(pl.multiple_of(block_at(i) * BCELLS, BCELLS), BCELLS)
        return remote(
            state.at[rows], x_buf.at[1, rows], sec_send.at[i], sec_recv.at[i], {"section": other}
        )

    def out_copy(i):
        rows = pl.ds(pl.multiple_of(block_at(i) * BCELLS, BCELLS), BCELLS)
        return pltpu.make_async_copy(final.at[rows], out.at[rows], out_sem.at[i])

    cell = iota((CELLS, 1), 0)
    land[...] = cell_column(
        land_sea[...].astype(F32), lax.shift_right_logical(cell, 4), cell & 15, CELLS
    )
    same = lax.shift_right_logical(iota((LANES, LANES), 0), 6) == lax.shift_right_logical(
        iota((LANES, LANES), 1), 6
    )
    ones_block[...] = jnp.where(same, 1.0, 0.0).astype(BF16)

    up_flag = has_up.astype(F32)
    down_flag = has_down.astype(F32)

    def build_flags():
        cell = iota((OWN, 1), 0)
        row = lax.shift_right_logical(cell, 4)
        col = cell & 15
        inside = cell_column(pole_mine[...], row - R, col, OWN)
        valid = jnp.where(row < R, up_flag, jnp.where(row >= R + ROWS, down_flag, inside))
        flag_own[...] = key_flags(row, col + R, valid, OWN)
        cell = iota((SIDE, 1), 0)
        row = jnp.floor((cell.astype(F32) + 0.5) * (1.0 / R)).astype(jnp.int32)
        col = cell - R * row
        row = row - (PROWS - R)
        for s, ref in ((0, flag_left), (1, flag_right)):
            picked = col + (COLS - R if s == 0 else 0)
            inside = cell_column(pole_side[s], row - R, picked, SIDE)
            valid = jnp.where(row < R, up_flag, jnp.where(row >= R + ROWS, down_flag, inside))
            ref[...] = key_flags(row, col + (0 if s == 0 else R + COLS), valid, SIDE)

    def unit(x):
        parts = []
        for t in range(GROUPS):
            part = x[:, t * LANES : (t + 1) * LANES]
            square = part * part
            high = square.astype(BF16)
            low = (square - high.astype(F32)).astype(BF16)
            total = dot(high, ones_block[...]) + dot(low, ones_block[...])
            parts.append((part * lax.rsqrt(total * (1.0 / HEAD) + 1e-06)).astype(BF16))
        return jnp.concatenate(parts, axis=1)

    def picker(first, count, cells, first_cell):
        line = iota((2 * count, cells), 0)
        side = (line >= count).astype(jnp.int32)
        strip_cell = line - count * side + first
        row = jnp.floor((strip_cell.astype(F32) + 0.5) * (1.0 / R)).astype(jnp.int32)
        wanted = row * COLS + (strip_cell - R * row) + (COLS - R) * side - first_cell
        return jnp.where(iota((2 * count, cells), 1) == wanted, 1.0, 0.0).astype(BF16)

    pick = picker(0, STRIP, PCELLS, 0)

    land_row = land_vector[...].reshape(1, D)
    lead_index = iota((lead_table.shape[0], 1), 0)
    lead_rows = [
        jnp.sum(
            jnp.where(lead_index == lead_steps[0, l], lead_table[...], 0.0), axis=0, keepdims=True
        )
        for l in (0, 1)
    ]

    def store_strips(l, picked, start, count, part, lanes):
        sent = dot(picked, part).astype(BF16)
        rows = pl.ds(pl.multiple_of(start, 16), count)
        strips[l, 0, rows, lanes] = sent[:count]
        strips[l, 1, rows, lanes] = sent[count:]

    def keys_values(l, start, size, done, before_value=lambda: None):
        rows = pl.ds(pl.multiple_of(start, BCELLS), size)
        cond = x_buf[l, rows, :].astype(F32) + lead_rows[l] + land[rows, :] * land_row
        mean_square = jnp.mean(cond * cond, axis=1, keepdims=True)
        flat = (cond * lax.rsqrt(mean_square + 1e-05) * norm_gain[...]).astype(BF16)
        normed[rows, :] = flat
        inner_rows = pl.ds(pl.multiple_of(start + R * COLS, 16), size)
        for weight, lanes in ((wk, pl.ds(0, INNER)), (wv, pl.ds(INNER, INNER))):
            if weight is wv:
                before_value()
            part = dot(flat, weight[...])
            part = unit(part) if weight is wk else part.astype(BF16)
            own[l, inner_rows, lanes] = part
            done(part, lanes)

    def piece_keys_values(l, p):
        c = piece_at(p)

        def done(part, lanes):
            store_strips(l, pick, c * STRIP, STRIP, part, lanes)

        def before_value():
            if l == 0:
                pl.when(p == 0)(load_value.wait)

        keys_values(l, c * PCELLS, PCELLS, done, before_value)
        if l == 0:
            pl.when(p < PIECES - 1)(lambda: start_z(l, p))
        else:
            start_z(l, p)

    def queries(start, size):
        rows = pl.ds(pl.multiple_of(start, BCELLS), size)
        query[rows, :] = unit(dot(normed[rows, :], wq[...]))

    def attend(l, i):
        b = block_at(i)
        rows = pl.ds(pl.multiple_of(b * BCELLS, BCELLS), BCELLS)
        own_rows = pl.ds(pl.multiple_of(b * BCELLS, BCELLS), 16 * COLS)
        side_rows = pl.ds(
            pl.multiple_of(16 * lax.shift_right_logical(6 * b + 3, 2), 16), REACH
        )
        spare = jnp.zeros((SPARE, LANES), BF16)
        q_cell = iota((BCELLS, WIDE), 0)
        lane = iota((BCELLS, WIDE), 1)
        q_row = lax.shift_right_logical(q_cell, 4) + b * BROWS
        q_col = q_cell & 15
        near_row = (lane >= q_row) & (lane <= q_row + 2 * R)
        near_col = (lane - 48 >= q_col) & (lane - 48 <= q_col + 2 * R)
        wanted = jnp.where(near_row | near_col | (lane == 100), 1.0, 0.0).astype(BF16)
        flags = jnp.concatenate(
            [flag_own[own_rows, :], flag_left[side_rows, :], flag_right[side_rows, :], spare[:, :WIDE]], axis=0
        )
        bias = jnp.where(dot_t(wanted, flags) > 2.5, 0.0, LOW)
        lane_head = lax.shift_right_logical(iota((1, LANES), 1), 6)
        for g in range(GROUPS):
            k_lanes = pl.ds(g * LANES, LANES)
            v_lanes = pl.ds(INNER + g * LANES, LANES)
            q = query[rows, k_lanes]
            q_all = jnp.concatenate(
                [
                    jnp.where(lane_head == h, q, jnp.zeros_like(q))
                    for h in range(PER_GROUP)
                ],
                axis=0,
            )
            keys = jnp.concatenate(
                [
                    own[l, own_rows, k_lanes],
                    left[l, side_rows, k_lanes],
                    right[l, side_rows, k_lanes],
                    spare,
                ],
                axis=0,
            )
            values = jnp.concatenate(
                [
                    own[l, own_rows, v_lanes],
                    left[l, side_rows, v_lanes],
                    right[l, side_rows, v_lanes],
                    spare,
                ],
                axis=0,
            )
            scores = dot_t(q_all, keys)
            probs = []
            inverses = []
            for h in range(PER_GROUP):
                factor = logit_scale[0, g * PER_GROUP + h] * (LOG2E / HEAD)
                part = scores[h * BCELLS : (h + 1) * BCELLS] * factor + bias
                prob = jnp.exp2(part - jnp.max(part, axis=1, keepdims=True))
                inverses.append(1.0 / jnp.sum(prob, axis=1, keepdims=True))
                probs.append(prob.astype(BF16))
            mixed = dot(jnp.concatenate(probs, axis=0), values)
            total = jnp.zeros((BCELLS, LANES), F32)
            for h in range(PER_GROUP):
                part = mixed[h * BCELLS : (h + 1) * BCELLS] * inverses[h]
                total = jnp.where(lane_head == h, part, total)
            attended[rows, k_lanes] = total.astype(BF16)

    def project_out(l, start, size):
        rows = pl.ds(pl.multiple_of(start, BCELLS), size)
        moved = x_buf[l, rows, :].astype(F32) + dot(attended[rows, :], wo[...])
        (state if l == 0 else final)[rows, :] = moved.astype(BF16)

    def order(i):
        return lax.rem(i + 2, 4) + 2 * lax.shift_right_logical(i, 2)

    load_key.wait()

    def first_project(p, carry):
        load_piece(p).wait()

        @pl.when(p == 1)
        def _():
            start_edge_own(0, 0)
            load_query.start()
            load_out.start()

        piece_keys_values(0, p)
        return carry

    pl.semaphore_wait(barrier, 3 + has_early.astype(jnp.int32) + has_late.astype(jnp.int32))
    for copy in pole_copies:
        copy.start()
    lax.fori_loop(0, PIECES, first_project, 0)
    start_z(0, PIECES)
    start_edge_own(0, 1)
    load_query.wait()

    def first_query(p, carry):
        queries(piece_at(p) * PCELLS, PCELLS)
        return carry

    lax.fori_loop(0, PIECES, first_query, 0)
    for p in (0, 1, PIECES):
        sent_z(0, p)
    start_z(0, PIECES + 1)
    start_corners(0)
    load_out.wait()
    for copy in pole_copies:
        copy.wait_recv()
    build_flags()
    wait_z(0, 0)
    wait_z(0, 1)
    wait_z(0, PIECES)

    def first_body(i, carry):
        block = order(i)

        @pl.when(i == 1)
        def _():
            wait_z(0, PIECES + 1)
            start_late_sides(0)

        @pl.when(i == 2)
        def _():
            wait_corners(0)

        @pl.when(i == 4)
        def _():
            wait_late(0)

        attend(0, block)

        @pl.when(i < 2)
        def _():
            project_out(0, block_at(block) * BCELLS, BCELLS)
            section_copy(block).start()

        @pl.when((i == 3) | (i == 5))
        def _():
            project_out(0, piece_at(lax.shift_right_logical(block, 1)) * PCELLS, PCELLS)

        return carry

    lax.fori_loop(0, BLOCKS, first_body, 0)

    def send_after(block, earlier):
        section_copy(earlier).wait_send()
        section_copy(block).start()

    def second_project(step, carry):
        p = 1 - step
        send_after(4 * step, 2 * p)
        send_after(4 * step + 1, 2 * p + 1)
        section_copy(2 * p).wait_recv()
        section_copy(2 * p + 1).wait_recv()
        piece_keys_values(1, p)

        @pl.when(step == 1)
        def _():
            start_edge_own(1, 0)

        queries(piece_at(p) * PCELLS, PCELLS)
        return carry

    lax.fori_loop(0, PIECES - 1, second_project, 0)

    def last_piece():
        c = piece_at(PIECES - 1)
        section_copy(4).wait_recv()
        block = block_at(4)
        start, count = part_at(PIECES)
        half = (block - 2 * c) * BCELLS
        picked = picker(start - c * STRIP, count, BCELLS, half)

        def done(part, lanes):
            store_strips(1, picked, start, count, part, lanes)

        keys_values(1, block * BCELLS, BCELLS, done)
        start_z(1, PIECES)
        queries(block * BCELLS, BCELLS)
        start_corners(1)

        section_copy(5).wait_recv()
        block = block_at(5)
        start, count = part_at(PIECES + 1)
        picked = picker(start - c * STRIP, count, PCELLS, 0)
        keys_values(1, block * BCELLS, BCELLS, lambda part, lanes: None)
        rows = pl.ds(pl.multiple_of(c * PCELLS + R * COLS, 16), PCELLS)
        for lanes in (pl.ds(0, INNER), pl.ds(INNER, INNER)):
            store_strips(1, picked, start, count, own[1, rows, lanes], lanes)
        start_z(1, PIECES + 1)
        start_edge_own(1, 1)
        queries(block * BCELLS, BCELLS)

    half_cells = CELLS // 2

    def second_body(i, carry):
        block = lax.rem(i + 2, 3) + 3 * lax.div(i, 3)
        block = jnp.where(i < 3, block, i)

        @pl.when(i == 1)
        def _():
            wait_corners(1)

        @pl.when(i == 3)
        def _():
            project_out(1, flip * half_cells, half_cells)
            for j in range(3):
                out_copy(j).start()
            wait_z(1, PIECES + 1)
            start_late_sides(1)

        @pl.when(i == 4)
        def _():
            wait_late(1)

        attend(1, block)
        return carry

    last_piece()
    wait_z(1, 1)
    wait_z(1, 0)
    wait_z(1, PIECES)
    lax.fori_loop(0, BLOCKS, second_body, 0)
    project_out(1, (1 - flip) * half_cells, half_cells)
    for j in range(3, BLOCKS):
        out_copy(j).start()

    for copy in pole_copies:
        copy.wait_send()
    for i in (4, 5):
        section_copy(i).wait_send()
    sent_z(0, PIECES + 1)
    for p in (0, 1, PIECES, PIECES + 1):
        sent_z(1, p)
    for l in (0, 1):

        def early_sent(l=l):
            edge_copies(l, 0, (0,))[0].wait_send()
            for copy in corner_copies(l):
                copy.wait_send()

        def late_sent(l=l):
            for copy in edge_copies(l, 1, (0, 1, 2)):
                copy.wait_send()

        edge_when(0, early_sent)
        edge_when(1, late_sent)
    for i in range(BLOCKS):
        out_copy(i).wait()


def per_device(
    lat_count,
    lon_count,
    fields,
    land_sea,
    pole_valid,
    lead_steps,
    lead_table,
    land_vector,
    norm_gain,
    w_query,
    w_key,
    w_value,
    w_out,
    logit_scale,
):
    smem = pl.BlockSpec(memory_space=pltpu.SMEM)
    hbm = pl.BlockSpec(memory_space=pl.ANY)
    result = pl.pallas_call(
        functools.partial(kernel, lat_count, lon_count),
        out_shape=jax.ShapeDtypeStruct((CELLS, D), BF16),
        in_specs=[smem, smem] + [hbm] * 10,
        out_specs=hbm,
        scratch_shapes=[
            pltpu.VMEM((COLS, ROWS), jnp.int32),
            pltpu.VMEM((COLS, ROWS), jnp.int32),
            pltpu.VMEM(lead_table.shape, F32),
            pltpu.VMEM(land_vector.shape, F32),
            pltpu.VMEM(norm_gain.shape, F32),
            pltpu.VMEM((2, CELLS, D), BF16),
            pltpu.VMEM((CELLS, D), BF16),
            pltpu.VMEM((CELLS, D), BF16),
            pltpu.VMEM((CELLS, D), BF16),
            pltpu.VMEM((D, INNER), BF16),
            pltpu.VMEM((D, INNER), BF16),
            pltpu.VMEM((D, INNER), BF16),
            pltpu.VMEM((INNER, D), BF16),
            pltpu.VMEM((CELLS, INNER), BF16),
            pltpu.VMEM((2, OWN, D), BF16),
            pltpu.VMEM((2, SIDE, D), BF16),
            pltpu.VMEM((2, SIDE, D), BF16),
            pltpu.VMEM((2, 2, PIECES * STRIP, D), BF16),
            pltpu.VMEM((OWN, WIDE), BF16),
            pltpu.VMEM((SIDE, WIDE), BF16),
            pltpu.VMEM((SIDE, WIDE), BF16),
            pltpu.VMEM((CELLS, 1), F32),
            pltpu.VMEM((CELLS, INNER), BF16),
            pltpu.VMEM((LANES, LANES), BF16),
            pltpu.VMEM((COLS, 128), F32),
            pltpu.VMEM((2, COLS, 128), F32),
            pltpu.VMEM((2, 2, STRIP, D), BF16),
            pltpu.SemaphoreType.DMA((5,)),
            pltpu.SemaphoreType.DMA((PIECES + 4,)),
            pltpu.SemaphoreType.DMA((BLOCKS,)),
            pltpu.SemaphoreType.DMA((2, SLOTS)),
            pltpu.SemaphoreType.DMA((2, SLOTS)),
            pltpu.SemaphoreType.DMA((BLOCKS,)),
            pltpu.SemaphoreType.DMA((BLOCKS,)),
            pltpu.SemaphoreType.DMA((2,)),
            pltpu.SemaphoreType.DMA((2,)),
        ],
        compiler_params=pltpu.CompilerParams(
            collective_id=0, has_side_effects=True, vmem_limit_bytes=56 * 1024 * 1024
        ),
    )(
        lead_steps,
        logit_scale,
        fields.reshape(CELLS, D),
        land_sea.T,
        pole_valid.T,
        lead_table,
        land_vector,
        norm_gain,
        w_query[0],
        w_key[0],
        w_value[0],
        w_out[0],
    )
    return result.reshape(1, ROWS, COLS, D)


def solution(mesh):
    return jax.shard_map(
        functools.partial(per_device, mesh.shape["lat"], mesh.shape["lon"]),
        mesh=mesh,
        in_specs=(
            P("section", "lat", "lon", None),
            P("lat", "lon"),
            P("lat", "lon"),
            P("section", None),
            P(),
            P(),
            P("section", None),
            P("section", None, None),
            P("section", None, None),
            P("section", None, None),
            P("section", None, None),
            P("section", None),
        ),
        out_specs=P("section", "lat", "lon", None),
        check_vma=False,
    )
```

```python
import functools

import jax
import jax.numpy as jnp
from jax import lax
from jax.experimental import pallas as pl
from jax.experimental.pallas import tpu as pltpu
from jax.sharding import PartitionSpec as P

R = 6
ROWS = 24
COLS = 16
CELLS = ROWS * COLS
D = 1536
INNER = 768
HEADS = 12
HEAD = 64
LANES = 256
GROUPS = INNER // LANES
PER_GROUP = LANES // HEAD
PROWS = 8
PCELLS = PROWS * COLS
PIECES = ROWS // PROWS
BROWS = 4
BCELLS = BROWS * COLS
BLOCKS = ROWS // BROWS
STRIP = PROWS * R
OWN = (ROWS + 2 * R) * COLS
SIDE = (ROWS + 2 * PROWS) * R
REACH = 112
SPARE = 32
WIDE = 128
LOG2E = 1.4426950408889634
LOW = -1e30
F32 = jnp.float32
BF16 = jnp.bfloat16

PARTS = PIECES + 2
EDGE = 2 * PARTS
SLOTS = EDGE + 6


def dot_t(a, b):
    return lax.dot_general(a, b, (((1,), (1,)), ((), ())), preferred_element_type=F32)


def dot(a, b):
    return jnp.dot(a, b, preferred_element_type=F32)


def iota(shape, dim):
    return lax.broadcasted_iota(jnp.int32, shape, dim)


def cell_column(grid, row, col, cells):
    picks = (iota((cells, grid.shape[0]), 1) == col).astype(F32).astype(BF16)
    found = dot(picks, grid.astype(BF16))
    hit = iota(found.shape, 1) == row
    return jnp.sum(jnp.where(hit, found, 0.0), axis=1, keepdims=True)


def key_flags(row, col, valid, cells):
    lane = iota((cells, WIDE), 1)
    hit = (lane == row) | (lane == col + 48)
    flags = jnp.where(lane == 100, valid, jnp.where(hit, 1.0, 0.0))
    return flags.astype(BF16)


def kernel(
    lat_count,
    lon_count,
    lead_steps,
    logit_scale,
    fields,
    land_sea_in,
    pole_valid_in,
    lead_table_in,
    land_vector_in,
    norm_gain_in,
    w_query,
    w_key,
    w_value,
    w_out,
    out,
    land_sea,
    pole_valid,
    lead_table,
    land_vector,
    norm_gain,
    x_buf,
    state,
    final,
    normed,
    wq,
    wk,
    wv,
    wo,
    query,
    own,
    left,
    right,
    strips,
    flag_own,
    flag_left,
    flag_right,
    land,
    attended,
    ones_block,
    pole_mine,
    pole_side,
    corners,
    biases,
    small_sem,
    load_sem,
    out_sem,
    send_sem,
    recv_sem,
    sec_send,
    sec_recv,
    pole_send,
    pole_recv,
):
    lat = lax.axis_index("lat")
    lon = lax.axis_index("lon")
    sec = lax.axis_index("section")
    west = lax.rem(lon + lon_count - 1, lon_count)
    east = lax.rem(lon + 1, lon_count)
    other = 1 - sec
    flip = lax.rem(lat, 2)
    has_up = lat > 0
    has_down = lat < lat_count - 1
    early = lat - 1 + 2 * flip
    late = lat + 1 - 2 * flip
    has_early = jnp.where(flip == 0, has_up, has_down)
    has_late = jnp.where(flip == 0, has_down, has_up)

    barrier = pltpu.get_barrier_semaphore()
    pl.semaphore_signal(barrier, inc=1, device_id={"lon": west})
    pl.semaphore_signal(barrier, inc=1, device_id={"lon": east})
    pl.semaphore_signal(barrier, inc=1, device_id={"section": other})

    @pl.when(has_early)
    def _():
        pl.semaphore_signal(barrier, inc=1, device_id={"lat": early})

    @pl.when(has_late)
    def _():
        pl.semaphore_signal(barrier, inc=1, device_id={"lat": late})

    def piece_at(p):
        return p + flip * (PIECES - 1 - 2 * p)

    def block_at(i):
        return i + flip * (BLOCKS - 1 - 2 * i)

    def load_piece(p):
        rows = pl.ds(pl.multiple_of(piece_at(p) * PCELLS, PCELLS), PCELLS)
        return pltpu.make_async_copy(fields.at[rows], x_buf.at[0, rows], load_sem.at[p])

    load_key = pltpu.make_async_copy(w_key, wk, load_sem.at[PIECES])
    load_value = pltpu.make_async_copy(w_value, wv, load_sem.at[PIECES + 1])
    load_query = pltpu.make_async_copy(w_query, wq, load_sem.at[PIECES + 2])
    load_out = pltpu.make_async_copy(w_out, wo, load_sem.at[PIECES + 3])
    load_piece(0).start()
    smalls = [
        pltpu.make_async_copy(src, dst, small_sem.at[i])
        for i, (src, dst) in enumerate(
            (
                (lead_table_in, lead_table),
                (land_vector_in, land_vector),
                (norm_gain_in, norm_gain),
                (land_sea_in, land_sea),
                (pole_valid_in, pole_valid),
            )
        )
    ]
    for small in smalls:
        small.start()
    load_key.start()
    load_value.start()
    for p in range(1, PIECES):
        load_piece(p).start()

    def clear_rows(missing, own_start, side_start):
        @pl.when(missing)
        def _():
            for l in (0, 1):
                own[l, pl.ds(own_start, R * COLS), :] = jnp.zeros((R * COLS, D), BF16)
                for buf in (left, right):
                    buf[l, pl.ds(side_start, STRIP), :] = jnp.zeros((STRIP, D), BF16)

    clear_rows(jnp.logical_not(has_up), 0, 0)
    clear_rows(jnp.logical_not(has_down), OWN - R * COLS, SIDE - STRIP)
    for small in smalls:
        small.wait()
    pole_mine[...] = jnp.zeros((COLS, 128), F32)
    pole_mine[:, pl.ds(0, ROWS)] = pole_valid[...].astype(F32)

    def remote(src, dst, send, recv, device):
        return pltpu.make_async_remote_copy(
            src_ref=src, dst_ref=dst, send_sem=send, recv_sem=recv, device_id=device
        )

    pole_copies = (
        remote(pole_mine, pole_side.at[1], pole_send.at[0], pole_recv.at[0], {"lon": west}),
        remote(pole_mine, pole_side.at[0], pole_send.at[1], pole_recv.at[1], {"lon": east}),
    )
    def part_at(p):
        if isinstance(p, int) and p >= PIECES:
            base = piece_at(PIECES - 1) * STRIP
            if p == PIECES:
                return base + flip * 32, 16
            return base + (1 - flip) * 16, 32
        return piece_at(p) * STRIP, STRIP

    def z_copies(l, p):
        start, size = part_at(p)
        src = pl.ds(pl.multiple_of(start, 16), size)
        dst = pl.ds(pl.multiple_of(start + STRIP, 16), size)
        return (
            remote(
                strips.at[l, 0, src],
                right.at[l, dst],
                send_sem.at[l, p],
                recv_sem.at[l, p],
                {"lon": west},
            ),
            remote(
                strips.at[l, 1, src],
                left.at[l, dst],
                send_sem.at[l, PARTS + p],
                recv_sem.at[l, PARTS + p],
                {"lon": east},
            ),
        )

    def start_z(l, p):
        for copy in z_copies(l, p):
            copy.start()

    def sent_z(l, p):
        for copy in z_copies(l, p):
            copy.wait_send()

    def edge_copies(l, which, parts):
        upper = flip if which else 1 - flip
        device = {"lat": late if which else early}
        base = EDGE + 3 * which
        o_src = pl.multiple_of((1 - upper) * (CELLS - R * COLS) + R * COLS, 16)
        o_dst = pl.multiple_of(upper * (OWN - R * COLS), 16)
        s_src = pl.multiple_of(STRIP + (1 - upper) * (PIECES - 1) * STRIP, 16)
        s_dst = pl.multiple_of(upper * (PIECES + 1) * STRIP, 16)
        copies = []
        for j in parts:
            buf = (own, left, right)[j]
            src, dst, size = (o_src, o_dst, R * COLS) if j == 0 else (s_src, s_dst, STRIP)
            copies.append(
                remote(
                    buf.at[l, pl.ds(src, size)],
                    buf.at[l, pl.ds(dst, size)],
                    send_sem.at[l, base + j],
                    recv_sem.at[l, base + j],
                    device,
                )
            )
        return copies

    def edge_when(which, act):
        pl.when(has_late if which else has_early)(act)

    def start_edge_own(l, which):
        def act():
            edge_copies(l, which, (0,))[0].start()

        edge_when(which, act)

    def start_late_sides(l):
        def act():
            for copy in edge_copies(l, 1, (1, 2)):
                copy.start()

        edge_when(1, act)

    def corner_copies(l):
        rows = pl.ds(pl.multiple_of(flip * (SIDE - STRIP), 16), STRIP)
        return (
            remote(
                corners.at[l, 0],
                right.at[l, rows],
                send_sem.at[l, EDGE + 1],
                recv_sem.at[l, EDGE + 1],
                {"lon": west},
            ),
            remote(
                corners.at[l, 1],
                left.at[l, rows],
                send_sem.at[l, EDGE + 2],
                recv_sem.at[l, EDGE + 2],
                {"lon": east},
            ),
        )

    def start_corners(l):
        def act():
            start = flip * (OWN - R * COLS)
            rows = pl.ds(pl.multiple_of(start, 16), R * COLS)
            ref = own.at[l, rows]
            remote(
                ref, ref, send_sem.at[l, EDGE], recv_sem.at[l, EDGE], {"lat": early}
            ).wait_recv()
            picked = picker(0, STRIP, R * COLS, (1 - flip) * (PROWS - R) * COLS)
            for lanes in (pl.ds(0, INNER), pl.ds(INNER, INNER)):
                sent = dot(picked, own[l, rows, lanes]).astype(BF16)
                corners[l, 0, :, lanes] = sent[:STRIP]
                corners[l, 1, :, lanes] = sent[STRIP:]
            for copy in corner_copies(l):
                copy.start()

        edge_when(0, act)

    def wait_corners(l):
        def act():
            for copy in corner_copies(l):
                copy.wait_recv()

        edge_when(0, act)

    def wait_late(l):
        o_dst = pl.multiple_of((1 - flip) * (OWN - R * COLS), 16)
        s_dst = pl.multiple_of((1 - flip) * (SIDE - STRIP), 16)

        def act():
            for j, (buf, start, size) in enumerate(
                ((own, o_dst, R * COLS), (left, s_dst, STRIP), (right, s_dst, STRIP))
            ):
                ref = buf.at[l, pl.ds(start, size)]
                remote(
                    ref,
                    ref,
                    send_sem.at[l, EDGE + 3 + j],
                    recv_sem.at[l, EDGE + 3 + j],
                    {"lat": late},
                ).wait_recv()

        edge_when(1, act)

    def wait_z(l, p):
        for copy in z_copies(l, p):
            copy.wait_recv()

    def section_copy(i):
        rows = pl.ds(pl.multiple_of(block_at(i) * BCELLS, BCELLS), BCELLS)
        return remote(
            state.at[rows], x_buf.at[1, rows], sec_send.at[i], sec_recv.at[i], {"section": other}
        )

    def out_copy(i):
        rows = pl.ds(pl.multiple_of(block_at(i) * BCELLS, BCELLS), BCELLS)
        return pltpu.make_async_copy(final.at[rows], out.at[rows], out_sem.at[i])

    cell = iota((CELLS, 1), 0)
    land[...] = cell_column(
        land_sea[...].astype(F32), lax.shift_right_logical(cell, 4), cell & 15, CELLS
    )
    same = lax.shift_right_logical(iota((LANES, LANES), 0), 6) == lax.shift_right_logical(
        iota((LANES, LANES), 1), 6
    )
    ones_block[...] = jnp.where(same, 1.0, 0.0).astype(BF16)

    up_flag = has_up.astype(F32)
    down_flag = has_down.astype(F32)

    def build_flags():
        cell = iota((OWN, 1), 0)
        row = lax.shift_right_logical(cell, 4)
        col = cell & 15
        inside = cell_column(pole_mine[...], row - R, col, OWN)
        valid = jnp.where(row < R, up_flag, jnp.where(row >= R + ROWS, down_flag, inside))
        flag_own[...] = key_flags(row, col + R, valid, OWN)
        cell = iota((SIDE, 1), 0)
        row = jnp.floor((cell.astype(F32) + 0.5) * (1.0 / R)).astype(jnp.int32)
        col = cell - R * row
        row = row - (PROWS - R)
        for s, ref in ((0, flag_left), (1, flag_right)):
            picked = col + (COLS - R if s == 0 else 0)
            inside = cell_column(pole_side[s], row - R, picked, SIDE)
            valid = jnp.where(row < R, up_flag, jnp.where(row >= R + ROWS, down_flag, inside))
            ref[...] = key_flags(row, col + (0 if s == 0 else R + COLS), valid, SIDE)

    def unit(x):
        parts = []
        for t in range(GROUPS):
            part = x[:, t * LANES : (t + 1) * LANES]
            square = part * part
            high = square.astype(BF16)
            low = (square - high.astype(F32)).astype(BF16)
            total = dot(high, ones_block[...]) + dot(low, ones_block[...])
            parts.append((part * lax.rsqrt(total * (1.0 / HEAD) + 1e-06)).astype(BF16))
        return jnp.concatenate(parts, axis=1)

    def picker(first, count, cells, first_cell):
        line = iota((2 * count, cells), 0)
        side = (line >= count).astype(jnp.int32)
        strip_cell = line - count * side + first
        row = jnp.floor((strip_cell.astype(F32) + 0.5) * (1.0 / R)).astype(jnp.int32)
        wanted = row * COLS + (strip_cell - R * row) + (COLS - R) * side - first_cell
        return jnp.where(iota((2 * count, cells), 1) == wanted, 1.0, 0.0).astype(BF16)

    pick = picker(0, STRIP, PCELLS, 0)

    land_row = land_vector[...].reshape(1, D)
    lead_index = iota((lead_table.shape[0], 1), 0)
    lead_rows = [
        jnp.sum(
            jnp.where(lead_index == lead_steps[0, l], lead_table[...], 0.0), axis=0, keepdims=True
        )
        for l in (0, 1)
    ]

    def store_strips(l, picked, start, count, part, lanes):
        sent = dot(picked, part).astype(BF16)
        rows = pl.ds(pl.multiple_of(start, 16), count)
        strips[l, 0, rows, lanes] = sent[:count]
        strips[l, 1, rows, lanes] = sent[count:]

    def keys_values(l, start, size, done, before_value=lambda: None):
        rows = pl.ds(pl.multiple_of(start, BCELLS), size)
        cond = x_buf[l, rows, :].astype(F32) + lead_rows[l] + land[rows, :] * land_row
        mean_square = jnp.mean(cond * cond, axis=1, keepdims=True)
        flat = (cond * lax.rsqrt(mean_square + 1e-05) * norm_gain[...]).astype(BF16)
        normed[rows, :] = flat
        inner_rows = pl.ds(pl.multiple_of(start + R * COLS, 16), size)
        for weight, lanes in ((wk, pl.ds(0, INNER)), (wv, pl.ds(INNER, INNER))):
            if weight is wv:
                before_value()
            part = dot(flat, weight[...])
            part = unit(part) if weight is wk else part.astype(BF16)
            own[l, inner_rows, lanes] = part
            done(part, lanes)

    def piece_keys_values(l, p):
        c = piece_at(p)

        def done(part, lanes):
            store_strips(l, pick, c * STRIP, STRIP, part, lanes)

        def before_value():
            if l == 0:
                pl.when(p == 0)(load_value.wait)

        keys_values(l, c * PCELLS, PCELLS, done, before_value)
        if l == 0:
            pl.when(p < PIECES - 1)(lambda: start_z(l, p))
        else:
            start_z(l, p)

    def queries(start, size):
        rows = pl.ds(pl.multiple_of(start, BCELLS), size)
        query[rows, :] = unit(dot(normed[rows, :], wq[...]))

    def key_rows(b):
        own_rows = pl.ds(pl.multiple_of(b * BCELLS, BCELLS), 16 * COLS)
        side = 16 * lax.shift_right_logical(6 * b + 3, 2)
        return own_rows, pl.ds(pl.multiple_of(side, 16), REACH)

    spare = jnp.zeros((SPARE, LANES), BF16)

    def build_bias(b, carry):
        own_rows, side_rows = key_rows(b)
        q_cell = iota((BCELLS, WIDE), 0)
        lane = iota((BCELLS, WIDE), 1)
        q_row = lax.shift_right_logical(q_cell, 4) + b * BROWS
        q_col = q_cell & 15
        near_row = (lane >= q_row) & (lane <= q_row + 2 * R)
        near_col = (lane - 48 >= q_col) & (lane - 48 <= q_col + 2 * R)
        wanted = jnp.where(near_row | near_col | (lane == 100), 1.0, 0.0).astype(BF16)
        flags = jnp.concatenate(
            [flag_own[own_rows, :], flag_left[side_rows, :], flag_right[side_rows, :], spare[:, :WIDE]], axis=0
        )
        biases[b] = jnp.where(dot_t(wanted, flags) > 2.5, 0.0, LOW)
        return carry

    def attend(l, i):
        b = block_at(i)
        rows = pl.ds(pl.multiple_of(b * BCELLS, BCELLS), BCELLS)
        own_rows, side_rows = key_rows(b)
        bias = biases[b]
        lane_head = lax.shift_right_logical(iota((1, LANES), 1), 6)
        for g in range(GROUPS):
            k_lanes = pl.ds(g * LANES, LANES)
            v_lanes = pl.ds(INNER + g * LANES, LANES)
            q = query[rows, k_lanes]
            q_all = jnp.concatenate(
                [
                    jnp.where(lane_head == h, q, jnp.zeros_like(q))
                    for h in range(PER_GROUP)
                ],
                axis=0,
            )
            keys = jnp.concatenate(
                [
                    own[l, own_rows, k_lanes],
                    left[l, side_rows, k_lanes],
                    right[l, side_rows, k_lanes],
                    spare,
                ],
                axis=0,
            )
            values = jnp.concatenate(
                [
                    own[l, own_rows, v_lanes],
                    left[l, side_rows, v_lanes],
                    right[l, side_rows, v_lanes],
                    spare,
                ],
                axis=0,
            )
            scores = dot_t(q_all, keys)
            probs = []
            inverses = []
            for h in range(PER_GROUP):
                factor = logit_scale[0, g * PER_GROUP + h] * (LOG2E / HEAD)
                part = scores[h * BCELLS : (h + 1) * BCELLS] * factor + bias
                prob = jnp.exp2(part - jnp.max(part, axis=1, keepdims=True))
                inverses.append(1.0 / jnp.sum(prob, axis=1, keepdims=True))
                probs.append(prob.astype(BF16))
            mixed = dot(jnp.concatenate(probs, axis=0), values)
            total = jnp.zeros((BCELLS, LANES), F32)
            for h in range(PER_GROUP):
                part = mixed[h * BCELLS : (h + 1) * BCELLS] * inverses[h]
                total = jnp.where(lane_head == h, part, total)
            attended[rows, k_lanes] = total.astype(BF16)

    def project_out(l, start, size):
        rows = pl.ds(pl.multiple_of(start, BCELLS), size)
        moved = x_buf[l, rows, :].astype(F32) + dot(attended[rows, :], wo[...])
        (state if l == 0 else final)[rows, :] = moved.astype(BF16)

    def order(i):
        return jnp.where(i < 3, lax.rem(i + 2, 3), i)

    load_key.wait()

    def first_project(p, carry):
        load_piece(p).wait()

        @pl.when(p == 1)
        def _():
            start_edge_own(0, 0)
            load_query.start()
            load_out.start()

        piece_keys_values(0, p)
        return carry

    pl.semaphore_wait(barrier, 3 + has_early.astype(jnp.int32) + has_late.astype(jnp.int32))
    for copy in pole_copies:
        copy.start()
    lax.fori_loop(0, PIECES, first_project, 0)
    start_z(0, PIECES)
    start_edge_own(0, 1)
    load_query.wait()

    def first_query(p, carry):
        queries(piece_at(p) * PCELLS, PCELLS)
        return carry

    lax.fori_loop(0, PIECES, first_query, 0)
    for p in (0, 1, PIECES):
        sent_z(0, p)
    start_z(0, PIECES + 1)
    start_corners(0)
    load_out.wait()
    for copy in pole_copies:
        copy.wait_recv()
    build_flags()
    lax.fori_loop(0, BLOCKS, build_bias, 0)
    wait_z(0, 0)
    wait_z(0, 1)
    wait_z(0, PIECES)

    def first_body(i, carry):
        block = order(i)

        @pl.when(i == 1)
        def _():
            wait_z(0, PIECES + 1)
            start_late_sides(0)

            wait_corners(0)

        @pl.when(i == 4)
        def _():
            wait_late(0)

        attend(0, block)

        @pl.when(i < 4)
        def _():
            project_out(0, block_at(block) * BCELLS, BCELLS)

        @pl.when(i < 3)
        def _():
            section_copy(block).start()

        @pl.when(i == 5)
        def _():
            project_out(0, piece_at(lax.shift_right_logical(block, 1)) * PCELLS, PCELLS)

        return carry

    lax.fori_loop(0, BLOCKS, first_body, 0)

    def send_after(block, earlier):
        section_copy(earlier).wait_send()
        section_copy(block).start()

    def second_project(step, carry):
        p = step

        @pl.when(step == 0)
        def _():
            send_after(3, 2)
            send_after(4, 0)

        @pl.when(step == 1)
        def _():
            send_after(5, 1)

        section_copy(2 * p).wait_recv()
        section_copy(2 * p + 1).wait_recv()
        piece_keys_values(1, p)

        @pl.when(step == 0)
        def _():
            start_edge_own(1, 0)

        queries(piece_at(p) * PCELLS, PCELLS)
        return carry

    lax.fori_loop(0, PIECES - 1, second_project, 0)

    def last_piece():
        c = piece_at(PIECES - 1)
        section_copy(4).wait_recv()
        block = block_at(4)
        start, count = part_at(PIECES)
        half = (block - 2 * c) * BCELLS
        picked = picker(start - c * STRIP, count, BCELLS, half)

        def done(part, lanes):
            store_strips(1, picked, start, count, part, lanes)

        keys_values(1, block * BCELLS, BCELLS, done)
        start_z(1, PIECES)
        queries(block * BCELLS, BCELLS)
        start_corners(1)

        section_copy(5).wait_recv()
        block = block_at(5)
        start, count = part_at(PIECES + 1)
        picked = picker(start - c * STRIP, count, PCELLS, 0)
        keys_values(1, block * BCELLS, BCELLS, lambda part, lanes: None)
        rows = pl.ds(pl.multiple_of(c * PCELLS + R * COLS, 16), PCELLS)
        for lanes in (pl.ds(0, INNER), pl.ds(INNER, INNER)):
            store_strips(1, picked, start, count, own[1, rows, lanes], lanes)
        start_z(1, PIECES + 1)
        start_edge_own(1, 1)
        queries(block * BCELLS, BCELLS)

    half_cells = CELLS // 2

    def second_body(i, carry):
        block = lax.rem(i + 2, 3) + 3 * lax.div(i, 3)
        block = jnp.where(i < 3, block, i)

        @pl.when(i == 1)
        def _():
            wait_corners(1)

        @pl.when(i == 3)
        def _():
            project_out(1, flip * half_cells, half_cells)
            for j in range(3):
                out_copy(j).start()
            wait_z(1, PIECES + 1)
            start_late_sides(1)

        @pl.when(i == 4)
        def _():
            wait_late(1)

        attend(1, block)
        return carry

    last_piece()
    wait_z(1, 1)
    wait_z(1, 0)
    wait_z(1, PIECES)
    lax.fori_loop(0, BLOCKS, second_body, 0)
    project_out(1, (1 - flip) * half_cells, half_cells)
    for j in range(3, BLOCKS):
        out_copy(j).start()

    for copy in pole_copies:
        copy.wait_send()
    for i in (3, 4, 5):
        section_copy(i).wait_send()
    sent_z(0, PIECES + 1)
    for p in (0, 1, PIECES, PIECES + 1):
        sent_z(1, p)
    for l in (0, 1):

        def early_sent(l=l):
            edge_copies(l, 0, (0,))[0].wait_send()
            for copy in corner_copies(l):
                copy.wait_send()

        def late_sent(l=l):
            for copy in edge_copies(l, 1, (0, 1, 2)):
                copy.wait_send()

        edge_when(0, early_sent)
        edge_when(1, late_sent)
    for i in range(BLOCKS):
        out_copy(i).wait()


def per_device(
    lat_count,
    lon_count,
    fields,
    land_sea,
    pole_valid,
    lead_steps,
    lead_table,
    land_vector,
    norm_gain,
    w_query,
    w_key,
    w_value,
    w_out,
    logit_scale,
):
    smem = pl.BlockSpec(memory_space=pltpu.SMEM)
    hbm = pl.BlockSpec(memory_space=pl.ANY)
    result = pl.pallas_call(
        functools.partial(kernel, lat_count, lon_count),
        out_shape=jax.ShapeDtypeStruct((CELLS, D), BF16),
        in_specs=[smem, smem] + [hbm] * 10,
        out_specs=hbm,
        scratch_shapes=[
            pltpu.VMEM((COLS, ROWS), jnp.int32),
            pltpu.VMEM((COLS, ROWS), jnp.int32),
            pltpu.VMEM(lead_table.shape, F32),
            pltpu.VMEM(land_vector.shape, F32),
            pltpu.VMEM(norm_gain.shape, F32),
            pltpu.VMEM((2, CELLS, D), BF16),
            pltpu.VMEM((CELLS, D), BF16),
            pltpu.VMEM((CELLS, D), BF16),
            pltpu.VMEM((CELLS, D), BF16),
            pltpu.VMEM((D, INNER), BF16),
            pltpu.VMEM((D, INNER), BF16),
            pltpu.VMEM((D, INNER), BF16),
            pltpu.VMEM((INNER, D), BF16),
            pltpu.VMEM((CELLS, INNER), BF16),
            pltpu.VMEM((2, OWN, D), BF16),
            pltpu.VMEM((2, SIDE, D), BF16),
            pltpu.VMEM((2, SIDE, D), BF16),
            pltpu.VMEM((2, 2, PIECES * STRIP, D), BF16),
            pltpu.VMEM((OWN, WIDE), BF16),
            pltpu.VMEM((SIDE, WIDE), BF16),
            pltpu.VMEM((SIDE, WIDE), BF16),
            pltpu.VMEM((CELLS, 1), F32),
            pltpu.VMEM((CELLS, INNER), BF16),
            pltpu.VMEM((LANES, LANES), BF16),
            pltpu.VMEM((COLS, 128), F32),
            pltpu.VMEM((2, COLS, 128), F32),
            pltpu.VMEM((2, 2, STRIP, D), BF16),
            pltpu.VMEM((BLOCKS, BCELLS, 512), F32),
            pltpu.SemaphoreType.DMA((5,)),
            pltpu.SemaphoreType.DMA((PIECES + 4,)),
            pltpu.SemaphoreType.DMA((BLOCKS,)),
            pltpu.SemaphoreType.DMA((2, SLOTS)),
            pltpu.SemaphoreType.DMA((2, SLOTS)),
            pltpu.SemaphoreType.DMA((BLOCKS,)),
            pltpu.SemaphoreType.DMA((BLOCKS,)),
            pltpu.SemaphoreType.DMA((2,)),
            pltpu.SemaphoreType.DMA((2,)),
        ],
        compiler_params=pltpu.CompilerParams(
            collective_id=0, has_side_effects=True, vmem_limit_bytes=56 * 1024 * 1024
        ),
    )(
        lead_steps,
        logit_scale,
        fields.reshape(CELLS, D),
        land_sea.T,
        pole_valid.T,
        lead_table,
        land_vector,
        norm_gain,
        w_query[0],
        w_key[0],
        w_value[0],
        w_out[0],
    )
    return result.reshape(1, ROWS, COLS, D)


def solution(mesh):
    return jax.shard_map(
        functools.partial(per_device, mesh.shape["lat"], mesh.shape["lon"]),
        mesh=mesh,
        in_specs=(
            P("section", "lat", "lon", None),
            P("lat", "lon"),
            P("lat", "lon"),
            P("section", None),
            P(),
            P(),
            P("section", None),
            P("section", None, None),
            P("section", None, None),
            P("section", None, None),
            P("section", None, None),
            P("section", None),
        ),
        out_specs=P("section", "lat", "lon", None),
        check_vma=False,
    )
```

```python
import functools

import jax
import jax.numpy as jnp
from jax import lax
from jax.experimental import pallas as pl
from jax.experimental.pallas import tpu as pltpu
from jax.sharding import PartitionSpec as P

R = 6
ROWS = 24
COLS = 16
CELLS = ROWS * COLS
D = 1536
INNER = 768
HEADS = 12
HEAD = 64
LANES = 256
GROUPS = INNER // LANES
PER_GROUP = LANES // HEAD
PROWS = 8
PCELLS = PROWS * COLS
PIECES = ROWS // PROWS
BROWS = 4
BCELLS = BROWS * COLS
BLOCKS = ROWS // BROWS
STRIP = PROWS * R
OWN = (ROWS + 2 * R) * COLS
SIDE = (ROWS + 2 * PROWS) * R
REACH = 112
SPARE = 32
WIDE = 128
LOG2E = 1.4426950408889634
LOW = -1e30
F32 = jnp.float32
BF16 = jnp.bfloat16

PARTS = PIECES + 2
EDGE = 2 * PARTS
SLOTS = EDGE + 6


def dot_t(a, b):
    return lax.dot_general(a, b, (((1,), (1,)), ((), ())), preferred_element_type=F32)


def dot(a, b):
    return jnp.dot(a, b, preferred_element_type=F32)


def iota(shape, dim):
    return lax.broadcasted_iota(jnp.int32, shape, dim)


def cell_column(grid, row, col, cells):
    picks = (iota((cells, grid.shape[0]), 1) == col).astype(F32).astype(BF16)
    found = dot(picks, grid.astype(BF16))
    hit = iota(found.shape, 1) == row
    return jnp.sum(jnp.where(hit, found, 0.0), axis=1, keepdims=True)


def key_flags(row, col, valid, cells):
    lane = iota((cells, WIDE), 1)
    hit = (lane == row) | (lane == col + 48)
    flags = jnp.where(lane == 100, valid, jnp.where(hit, 1.0, 0.0))
    return flags.astype(BF16)


def kernel(
    lat_count,
    lon_count,
    lead_steps,
    logit_scale,
    fields,
    land_sea_in,
    pole_valid_in,
    lead_table_in,
    land_vector_in,
    norm_gain_in,
    w_query,
    w_key,
    w_value,
    w_out,
    out,
    land_sea,
    pole_valid,
    lead_table,
    land_vector,
    norm_gain,
    x_buf,
    state,
    final,
    normed,
    wq,
    wk,
    wv,
    wo,
    query,
    own,
    left,
    right,
    strips,
    flag_own,
    flag_left,
    flag_right,
    land,
    attended,
    ones_block,
    pole_mine,
    pole_side,
    corners,
    biases,
    small_sem,
    load_sem,
    out_sem,
    send_sem,
    recv_sem,
    sec_send,
    sec_recv,
    pole_send,
    pole_recv,
):
    lat = lax.axis_index("lat")
    lon = lax.axis_index("lon")
    sec = lax.axis_index("section")
    west = lax.rem(lon + lon_count - 1, lon_count)
    east = lax.rem(lon + 1, lon_count)
    other = 1 - sec
    flip = lax.rem(lat, 2)
    has_up = lat > 0
    has_down = lat < lat_count - 1
    early = lat - 1 + 2 * flip
    late = lat + 1 - 2 * flip
    has_early = jnp.where(flip == 0, has_up, has_down)
    has_late = jnp.where(flip == 0, has_down, has_up)

    barrier = pltpu.get_barrier_semaphore()
    pl.semaphore_signal(barrier, inc=1, device_id={"lon": west})
    pl.semaphore_signal(barrier, inc=1, device_id={"lon": east})
    pl.semaphore_signal(barrier, inc=1, device_id={"section": other})

    @pl.when(has_early)
    def _():
        pl.semaphore_signal(barrier, inc=1, device_id={"lat": early})

    @pl.when(has_late)
    def _():
        pl.semaphore_signal(barrier, inc=1, device_id={"lat": late})

    def piece_at(p):
        return p + flip * (PIECES - 1 - 2 * p)

    def block_at(i):
        return i + flip * (BLOCKS - 1 - 2 * i)

    def load_piece(p):
        rows = pl.ds(pl.multiple_of(piece_at(p) * PCELLS, PCELLS), PCELLS)
        return pltpu.make_async_copy(fields.at[rows], x_buf.at[0, rows], load_sem.at[p])

    load_key = pltpu.make_async_copy(w_key, wk, load_sem.at[PIECES])
    load_value = pltpu.make_async_copy(w_value, wv, load_sem.at[PIECES + 1])
    load_query = pltpu.make_async_copy(w_query, wq, load_sem.at[PIECES + 2])
    load_out = pltpu.make_async_copy(w_out, wo, load_sem.at[PIECES + 3])
    load_piece(0).start()
    smalls = [
        pltpu.make_async_copy(src, dst, small_sem.at[i])
        for i, (src, dst) in enumerate(
            (
                (lead_table_in, lead_table),
                (land_vector_in, land_vector),
                (norm_gain_in, norm_gain),
                (land_sea_in, land_sea),
                (pole_valid_in, pole_valid),
            )
        )
    ]
    for small in smalls:
        small.start()
    load_key.start()
    load_value.start()
    for p in range(1, PIECES):
        load_piece(p).start()

    def clear_rows(missing, own_start, side_start):
        @pl.when(missing)
        def _():
            for l in (0, 1):
                own[l, pl.ds(own_start, R * COLS), :] = jnp.zeros((R * COLS, D), BF16)
                for buf in (left, right):
                    buf[l, pl.ds(side_start, STRIP), :] = jnp.zeros((STRIP, D), BF16)

    clear_rows(jnp.logical_not(has_up), 0, 0)
    clear_rows(jnp.logical_not(has_down), OWN - R * COLS, SIDE - STRIP)
    for small in smalls:
        small.wait()
    pole_mine[...] = jnp.zeros((COLS, 128), F32)
    pole_mine[:, pl.ds(0, ROWS)] = pole_valid[...].astype(F32)

    def remote(src, dst, send, recv, device):
        return pltpu.make_async_remote_copy(
            src_ref=src, dst_ref=dst, send_sem=send, recv_sem=recv, device_id=device
        )

    pole_copies = (
        remote(pole_mine, pole_side.at[1], pole_send.at[0], pole_recv.at[0], {"lon": west}),
        remote(pole_mine, pole_side.at[0], pole_send.at[1], pole_recv.at[1], {"lon": east}),
    )
    def part_at(p):
        if isinstance(p, int) and p >= PIECES:
            base = piece_at(PIECES - 1) * STRIP
            if p == PIECES:
                return base + flip * 32, 16
            return base + (1 - flip) * 16, 32
        return piece_at(p) * STRIP, STRIP

    def z_copies(l, p):
        start, size = part_at(p)
        src = pl.ds(pl.multiple_of(start, 16), size)
        dst = pl.ds(pl.multiple_of(start + STRIP, 16), size)
        return (
            remote(
                strips.at[l, 0, src],
                right.at[l, dst],
                send_sem.at[l, p],
                recv_sem.at[l, p],
                {"lon": west},
            ),
            remote(
                strips.at[l, 1, src],
                left.at[l, dst],
                send_sem.at[l, PARTS + p],
                recv_sem.at[l, PARTS + p],
                {"lon": east},
            ),
        )

    def start_z(l, p):
        for copy in z_copies(l, p):
            copy.start()

    def sent_z(l, p):
        for copy in z_copies(l, p):
            copy.wait_send()

    def edge_copies(l, which, parts):
        upper = flip if which else 1 - flip
        device = {"lat": late if which else early}
        base = EDGE + 3 * which
        o_src = pl.multiple_of((1 - upper) * (CELLS - R * COLS) + R * COLS, 16)
        o_dst = pl.multiple_of(upper * (OWN - R * COLS), 16)
        s_src = pl.multiple_of(STRIP + (1 - upper) * (PIECES - 1) * STRIP, 16)
        s_dst = pl.multiple_of(upper * (PIECES + 1) * STRIP, 16)
        copies = []
        for j in parts:
            buf = (own, left, right)[j]
            src, dst, size = (o_src, o_dst, R * COLS) if j == 0 else (s_src, s_dst, STRIP)
            copies.append(
                remote(
                    buf.at[l, pl.ds(src, size)],
                    buf.at[l, pl.ds(dst, size)],
                    send_sem.at[l, base + j],
                    recv_sem.at[l, base + j],
                    device,
                )
            )
        return copies

    def edge_when(which, act):
        pl.when(has_late if which else has_early)(act)

    def start_edge_own(l, which):
        def act():
            edge_copies(l, which, (0,))[0].start()

        edge_when(which, act)

    def start_late_sides(l):
        def act():
            for copy in edge_copies(l, 1, (1, 2)):
                copy.start()

        edge_when(1, act)

    def corner_copies(l):
        rows = pl.ds(pl.multiple_of(flip * (SIDE - STRIP), 16), STRIP)
        return (
            remote(
                corners.at[l, 0],
                right.at[l, rows],
                send_sem.at[l, EDGE + 1],
                recv_sem.at[l, EDGE + 1],
                {"lon": west},
            ),
            remote(
                corners.at[l, 1],
                left.at[l, rows],
                send_sem.at[l, EDGE + 2],
                recv_sem.at[l, EDGE + 2],
                {"lon": east},
            ),
        )

    def start_corners(l):
        def act():
            start = flip * (OWN - R * COLS)
            rows = pl.ds(pl.multiple_of(start, 16), R * COLS)
            ref = own.at[l, rows]
            remote(
                ref, ref, send_sem.at[l, EDGE], recv_sem.at[l, EDGE], {"lat": early}
            ).wait_recv()
            picked = picker(0, STRIP, R * COLS, (1 - flip) * (PROWS - R) * COLS)
            for lanes in (pl.ds(0, INNER), pl.ds(INNER, INNER)):
                sent = dot(picked, own[l, rows, lanes]).astype(BF16)
                corners[l, 0, :, lanes] = sent[:STRIP]
                corners[l, 1, :, lanes] = sent[STRIP:]
            for copy in corner_copies(l):
                copy.start()

        edge_when(0, act)

    def wait_corners(l):
        def act():
            for copy in corner_copies(l):
                copy.wait_recv()

        edge_when(0, act)

    def wait_late(l):
        o_dst = pl.multiple_of((1 - flip) * (OWN - R * COLS), 16)
        s_dst = pl.multiple_of((1 - flip) * (SIDE - STRIP), 16)

        def act():
            for j, (buf, start, size) in enumerate(
                ((own, o_dst, R * COLS), (left, s_dst, STRIP), (right, s_dst, STRIP))
            ):
                ref = buf.at[l, pl.ds(start, size)]
                remote(
                    ref,
                    ref,
                    send_sem.at[l, EDGE + 3 + j],
                    recv_sem.at[l, EDGE + 3 + j],
                    {"lat": late},
                ).wait_recv()

        edge_when(1, act)

    def wait_z(l, p):
        for copy in z_copies(l, p):
            copy.wait_recv()

    def section_copy(i):
        rows = pl.ds(pl.multiple_of(block_at(i) * BCELLS, BCELLS), BCELLS)
        return remote(
            state.at[rows], x_buf.at[1, rows], sec_send.at[i], sec_recv.at[i], {"section": other}
        )

    def out_copy(i):
        rows = pl.ds(pl.multiple_of(block_at(i) * BCELLS, BCELLS), BCELLS)
        return pltpu.make_async_copy(final.at[rows], out.at[rows], out_sem.at[i])

    cell = iota((CELLS, 1), 0)
    land[...] = cell_column(
        land_sea[...].astype(F32), lax.shift_right_logical(cell, 4), cell & 15, CELLS
    )
    same = lax.shift_right_logical(iota((LANES, LANES), 0), 6) == lax.shift_right_logical(
        iota((LANES, LANES), 1), 6
    )
    ones_block[...] = jnp.where(same, 1.0, 0.0).astype(BF16)

    up_flag = has_up.astype(F32)
    down_flag = has_down.astype(F32)

    def build_flags():
        cell = iota((OWN, 1), 0)
        row = lax.shift_right_logical(cell, 4)
        col = cell & 15
        inside = cell_column(pole_mine[...], row - R, col, OWN)
        valid = jnp.where(row < R, up_flag, jnp.where(row >= R + ROWS, down_flag, inside))
        flag_own[...] = key_flags(row, col + R, valid, OWN)
        cell = iota((SIDE, 1), 0)
        row = jnp.floor((cell.astype(F32) + 0.5) * (1.0 / R)).astype(jnp.int32)
        col = cell - R * row
        row = row - (PROWS - R)
        for s, ref in ((0, flag_left), (1, flag_right)):
            picked = col + (COLS - R if s == 0 else 0)
            inside = cell_column(pole_side[s], row - R, picked, SIDE)
            valid = jnp.where(row < R, up_flag, jnp.where(row >= R + ROWS, down_flag, inside))
            ref[...] = key_flags(row, col + (0 if s == 0 else R + COLS), valid, SIDE)

    def unit(x):
        parts = []
        for t in range(GROUPS):
            part = x[:, t * LANES : (t + 1) * LANES]
            square = part * part
            high = square.astype(BF16)
            low = (square - high.astype(F32)).astype(BF16)
            total = dot(high, ones_block[...]) + dot(low, ones_block[...])
            parts.append((part * lax.rsqrt(total * (1.0 / HEAD) + 1e-06)).astype(BF16))
        return jnp.concatenate(parts, axis=1)

    def picker(first, count, cells, first_cell):
        line = iota((2 * count, cells), 0)
        side = (line >= count).astype(jnp.int32)
        strip_cell = line - count * side + first
        row = jnp.floor((strip_cell.astype(F32) + 0.5) * (1.0 / R)).astype(jnp.int32)
        wanted = row * COLS + (strip_cell - R * row) + (COLS - R) * side - first_cell
        return jnp.where(iota((2 * count, cells), 1) == wanted, 1.0, 0.0).astype(BF16)

    pick = picker(0, STRIP, PCELLS, 0)

    land_row = land_vector[...].reshape(1, D)
    lead_index = iota((lead_table.shape[0], 1), 0)
    lead_rows = [
        jnp.sum(
            jnp.where(lead_index == lead_steps[0, l], lead_table[...], 0.0), axis=0, keepdims=True
        )
        for l in (0, 1)
    ]

    def store_strips(l, picked, start, count, part, lanes):
        sent = dot(picked, part).astype(BF16)
        rows = pl.ds(pl.multiple_of(start, 16), count)
        strips[l, 0, rows, lanes] = sent[:count]
        strips[l, 1, rows, lanes] = sent[count:]

    def keys_values(l, start, size, done, before_value=lambda: None):
        rows = pl.ds(pl.multiple_of(start, BCELLS), size)
        cond = x_buf[l, rows, :].astype(F32) + lead_rows[l] + land[rows, :] * land_row
        mean_square = jnp.mean(cond * cond, axis=1, keepdims=True)
        flat = (cond * lax.rsqrt(mean_square + 1e-05) * norm_gain[...]).astype(BF16)
        normed[rows, :] = flat
        inner_rows = pl.ds(pl.multiple_of(start + R * COLS, 16), size)
        for weight, lanes in ((wk, pl.ds(0, INNER)), (wv, pl.ds(INNER, INNER))):
            if weight is wv:
                before_value()
            part = dot(flat, weight[...])
            part = unit(part) if weight is wk else part.astype(BF16)
            own[l, inner_rows, lanes] = part
            done(part, lanes)

    def piece_keys_values(l, p):
        c = piece_at(p)

        def done(part, lanes):
            store_strips(l, pick, c * STRIP, STRIP, part, lanes)

        def before_value():
            if l == 0:
                pl.when(p == 0)(load_value.wait)

        keys_values(l, c * PCELLS, PCELLS, done, before_value)
        if l == 0:
            pl.when(p < PIECES - 1)(lambda: start_z(l, p))
        else:
            start_z(l, p)

    def queries(start, size):
        rows = pl.ds(pl.multiple_of(start, BCELLS), size)
        query[rows, :] = unit(dot(normed[rows, :], wq[...]))

    def key_rows(b):
        own_rows = pl.ds(pl.multiple_of(b * BCELLS, BCELLS), 16 * COLS)
        side = 16 * lax.shift_right_logical(6 * b + 3, 2)
        return own_rows, pl.ds(pl.multiple_of(side, 16), REACH)

    spare = jnp.zeros((SPARE, LANES), BF16)

    def build_bias(b, carry):
        own_rows, side_rows = key_rows(b)
        q_cell = iota((BCELLS, WIDE), 0)
        lane = iota((BCELLS, WIDE), 1)
        q_row = lax.shift_right_logical(q_cell, 4) + b * BROWS
        q_col = q_cell & 15
        near_row = (lane >= q_row) & (lane <= q_row + 2 * R)
        near_col = (lane - 48 >= q_col) & (lane - 48 <= q_col + 2 * R)
        wanted = jnp.where(near_row | near_col | (lane == 100), 1.0, 0.0).astype(BF16)
        flags = jnp.concatenate(
            [flag_own[own_rows, :], flag_left[side_rows, :], flag_right[side_rows, :], spare[:, :WIDE]], axis=0
        )
        biases[b] = jnp.where(dot_t(wanted, flags) > 2.5, 0.0, LOW)
        return carry

    def attend(l, i):
        b = block_at(i)
        rows = pl.ds(pl.multiple_of(b * BCELLS, BCELLS), BCELLS)
        own_rows, side_rows = key_rows(b)
        bias = biases[b]
        lane_head = lax.shift_right_logical(iota((1, LANES), 1), 6)
        for g in range(GROUPS):
            k_lanes = pl.ds(g * LANES, LANES)
            v_lanes = pl.ds(INNER + g * LANES, LANES)
            q = query[rows, k_lanes]
            q_all = jnp.concatenate(
                [
                    jnp.where(lane_head == h, q, jnp.zeros_like(q))
                    for h in range(PER_GROUP)
                ],
                axis=0,
            )
            keys = jnp.concatenate(
                [
                    own[l, own_rows, k_lanes],
                    left[l, side_rows, k_lanes],
                    right[l, side_rows, k_lanes],
                    spare,
                ],
                axis=0,
            )
            values = jnp.concatenate(
                [
                    own[l, own_rows, v_lanes],
                    left[l, side_rows, v_lanes],
                    right[l, side_rows, v_lanes],
                    spare,
                ],
                axis=0,
            )
            scores = dot_t(q_all, keys)
            probs = []
            inverses = []
            for h in range(PER_GROUP):
                factor = logit_scale[0, g * PER_GROUP + h] * (LOG2E / HEAD)
                part = scores[h * BCELLS : (h + 1) * BCELLS] * factor + bias
                prob = jnp.exp2(part - jnp.max(part, axis=1, keepdims=True))
                inverses.append(1.0 / jnp.sum(prob, axis=1, keepdims=True))
                probs.append(prob.astype(BF16))
            mixed = dot(jnp.concatenate(probs, axis=0), values)
            total = jnp.zeros((BCELLS, LANES), F32)
            for h in range(PER_GROUP):
                part = mixed[h * BCELLS : (h + 1) * BCELLS] * inverses[h]
                total = jnp.where(lane_head == h, part, total)
            attended[rows, k_lanes] = total.astype(BF16)

    def project_out(l, start, size):
        rows = pl.ds(pl.multiple_of(start, BCELLS), size)
        moved = x_buf[l, rows, :].astype(F32) + dot(attended[rows, :], wo[...])
        (state if l == 0 else final)[rows, :] = moved.astype(BF16)

    def order(i):
        return jnp.where(i < 3, lax.rem(i + 2, 3), i)

    load_key.wait()

    def first_project(p, carry):
        load_piece(p).wait()

        @pl.when(p == 1)
        def _():
            start_edge_own(0, 0)
            load_query.start()
            load_out.start()

        piece_keys_values(0, p)
        return carry

    pl.semaphore_wait(barrier, 3 + has_early.astype(jnp.int32) + has_late.astype(jnp.int32))
    for copy in pole_copies:
        copy.start()
    lax.fori_loop(0, PIECES, first_project, 0)
    start_z(0, PIECES)
    start_edge_own(0, 1)
    load_query.wait()

    def first_query(p, carry):
        queries(piece_at(p) * PCELLS, PCELLS)
        return carry

    lax.fori_loop(0, PIECES, first_query, 0)
    for copy in pole_copies:
        copy.wait_recv()
    build_flags()
    for p in (0, 1, PIECES):
        sent_z(0, p)
    start_z(0, PIECES + 1)
    start_corners(0)
    lax.fori_loop(0, BLOCKS, build_bias, 0)
    load_out.wait()
    wait_z(0, 0)
    wait_z(0, 1)
    wait_z(0, PIECES)

    def first_body(i, carry):
        block = order(i)

        @pl.when(i == 1)
        def _():
            wait_z(0, PIECES + 1)
            start_late_sides(0)

            wait_corners(0)

        @pl.when(i == 4)
        def _():
            wait_late(0)

        attend(0, block)

        @pl.when(i < 4)
        def _():
            project_out(0, block_at(block) * BCELLS, BCELLS)

        @pl.when(i < 3)
        def _():
            section_copy(block).start()

        @pl.when(i == 5)
        def _():
            project_out(0, piece_at(lax.shift_right_logical(block, 1)) * PCELLS, PCELLS)

        return carry

    lax.fori_loop(0, BLOCKS, first_body, 0)

    def send_after(block, earlier):
        section_copy(earlier).wait_send()
        section_copy(block).start()

    def second_project(step, carry):
        p = step

        @pl.when(step == 0)
        def _():
            send_after(3, 2)
            send_after(4, 0)

        @pl.when(step == 1)
        def _():
            send_after(5, 1)

        section_copy(2 * p).wait_recv()
        section_copy(2 * p + 1).wait_recv()
        piece_keys_values(1, p)

        @pl.when(step == 0)
        def _():
            start_edge_own(1, 0)

        queries(piece_at(p) * PCELLS, PCELLS)
        return carry

    lax.fori_loop(0, PIECES - 1, second_project, 0)

    def last_piece():
        c = piece_at(PIECES - 1)
        section_copy(4).wait_recv()
        block = block_at(4)
        start, count = part_at(PIECES)
        half = (block - 2 * c) * BCELLS
        picked = picker(start - c * STRIP, count, BCELLS, half)

        def done(part, lanes):
            store_strips(1, picked, start, count, part, lanes)

        keys_values(1, block * BCELLS, BCELLS, done)
        start_z(1, PIECES)
        queries(block * BCELLS, BCELLS)
        start_corners(1)

        section_copy(5).wait_recv()
        block = block_at(5)
        start, count = part_at(PIECES + 1)
        picked = picker(start - c * STRIP, count, PCELLS, 0)
        keys_values(1, block * BCELLS, BCELLS, lambda part, lanes: None)
        rows = pl.ds(pl.multiple_of(c * PCELLS + R * COLS, 16), PCELLS)
        for lanes in (pl.ds(0, INNER), pl.ds(INNER, INNER)):
            store_strips(1, picked, start, count, own[1, rows, lanes], lanes)
        start_z(1, PIECES + 1)
        start_edge_own(1, 1)
        queries(block * BCELLS, BCELLS)

    half_cells = CELLS // 2

    def second_body(i, carry):
        block = lax.rem(i + 2, 3) + 3 * lax.div(i, 3)
        block = jnp.where(i < 3, block, i)

        @pl.when(i == 1)
        def _():
            wait_corners(1)

        @pl.when(i == 3)
        def _():
            project_out(1, flip * half_cells, half_cells)
            for j in range(3):
                out_copy(j).start()
            wait_z(1, PIECES + 1)
            start_late_sides(1)

        @pl.when(i == 4)
        def _():
            wait_late(1)

        attend(1, block)
        return carry

    last_piece()
    wait_z(1, 1)
    wait_z(1, 0)
    wait_z(1, PIECES)
    lax.fori_loop(0, BLOCKS, second_body, 0)
    project_out(1, (1 - flip) * half_cells, half_cells)
    for j in range(3, BLOCKS):
        out_copy(j).start()

    for copy in pole_copies:
        copy.wait_send()
    for i in (3, 4, 5):
        section_copy(i).wait_send()
    sent_z(0, PIECES + 1)
    for p in (0, 1, PIECES, PIECES + 1):
        sent_z(1, p)
    for l in (0, 1):

        def early_sent(l=l):
            edge_copies(l, 0, (0,))[0].wait_send()
            for copy in corner_copies(l):
                copy.wait_send()

        def late_sent(l=l):
            for copy in edge_copies(l, 1, (0, 1, 2)):
                copy.wait_send()

        edge_when(0, early_sent)
        edge_when(1, late_sent)
    for i in range(BLOCKS):
        out_copy(i).wait()


def per_device(
    lat_count,
    lon_count,
    fields,
    land_sea,
    pole_valid,
    lead_steps,
    lead_table,
    land_vector,
    norm_gain,
    w_query,
    w_key,
    w_value,
    w_out,
    logit_scale,
):
    smem = pl.BlockSpec(memory_space=pltpu.SMEM)
    hbm = pl.BlockSpec(memory_space=pl.ANY)
    result = pl.pallas_call(
        functools.partial(kernel, lat_count, lon_count),
        out_shape=jax.ShapeDtypeStruct((CELLS, D), BF16),
        in_specs=[smem, smem] + [hbm] * 10,
        out_specs=hbm,
        scratch_shapes=[
            pltpu.VMEM((COLS, ROWS), jnp.int32),
            pltpu.VMEM((COLS, ROWS), jnp.int32),
            pltpu.VMEM(lead_table.shape, F32),
            pltpu.VMEM(land_vector.shape, F32),
            pltpu.VMEM(norm_gain.shape, F32),
            pltpu.VMEM((2, CELLS, D), BF16),
            pltpu.VMEM((CELLS, D), BF16),
            pltpu.VMEM((CELLS, D), BF16),
            pltpu.VMEM((CELLS, D), BF16),
            pltpu.VMEM((D, INNER), BF16),
            pltpu.VMEM((D, INNER), BF16),
            pltpu.VMEM((D, INNER), BF16),
            pltpu.VMEM((INNER, D), BF16),
            pltpu.VMEM((CELLS, INNER), BF16),
            pltpu.VMEM((2, OWN, D), BF16),
            pltpu.VMEM((2, SIDE, D), BF16),
            pltpu.VMEM((2, SIDE, D), BF16),
            pltpu.VMEM((2, 2, PIECES * STRIP, D), BF16),
            pltpu.VMEM((OWN, WIDE), BF16),
            pltpu.VMEM((SIDE, WIDE), BF16),
            pltpu.VMEM((SIDE, WIDE), BF16),
            pltpu.VMEM((CELLS, 1), F32),
            pltpu.VMEM((CELLS, INNER), BF16),
            pltpu.VMEM((LANES, LANES), BF16),
            pltpu.VMEM((COLS, 128), F32),
            pltpu.VMEM((2, COLS, 128), F32),
            pltpu.VMEM((2, 2, STRIP, D), BF16),
            pltpu.VMEM((BLOCKS, BCELLS, 512), F32),
            pltpu.SemaphoreType.DMA((5,)),
            pltpu.SemaphoreType.DMA((PIECES + 4,)),
            pltpu.SemaphoreType.DMA((BLOCKS,)),
            pltpu.SemaphoreType.DMA((2, SLOTS)),
            pltpu.SemaphoreType.DMA((2, SLOTS)),
            pltpu.SemaphoreType.DMA((BLOCKS,)),
            pltpu.SemaphoreType.DMA((BLOCKS,)),
            pltpu.SemaphoreType.DMA((2,)),
            pltpu.SemaphoreType.DMA((2,)),
        ],
        compiler_params=pltpu.CompilerParams(
            collective_id=0, has_side_effects=True, vmem_limit_bytes=56 * 1024 * 1024
        ),
    )(
        lead_steps,
        logit_scale,
        fields.reshape(CELLS, D),
        land_sea.T,
        pole_valid.T,
        lead_table,
        land_vector,
        norm_gain,
        w_query[0],
        w_key[0],
        w_value[0],
        w_out[0],
    )
    return result.reshape(1, ROWS, COLS, D)


def solution(mesh):
    return jax.shard_map(
        functools.partial(per_device, mesh.shape["lat"], mesh.shape["lon"]),
        mesh=mesh,
        in_specs=(
            P("section", "lat", "lon", None),
            P("lat", "lon"),
            P("lat", "lon"),
            P("section", None),
            P(),
            P(),
            P("section", None),
            P("section", None, None),
            P("section", None, None),
            P("section", None, None),
            P("section", None, None),
            P("section", None),
        ),
        out_specs=P("section", "lat", "lon", None),
        check_vma=False,
    )
```
